512 devices in a mesh: replica: 16 (over z, core), table: 32 (over x, y).
Axes of the slice: x: 4, y: 8, z: 8, core: 2. Of those that a mesh axis runs over, the one named last changes fastest.
Arguments:
- table: float32 [32768, 128], P('table'), may hold values from -0.6 to 0.6
- row_state: float32 [32768], P('table'), may hold values from 1.1920929e-08 to 2.3841858e-07
- lookup_grads: bfloat16 [16, 32768, 128], P('replica', 'table'), may hold values from -6 to 6
- lookup_slots: int32 [16, 32768], P('replica', 'table'), may hold values from 0 to 3
- lookup_rows: int32 [16, 32768], P('replica', 'table'), may hold values from 0 to 127
- block_ids: int32 [16, 128], P('replica', 'table'), may hold values from 0 to 7, as said below
- block_counts: int32 [16, 32], P('replica', 'table'), may hold values from 1 to 4, as said below
- inputs: bfloat16 [524288, 512], P(('replica', 'table')), may hold values from -2036.4675 to 2036.4675
- cotangent: bfloat16 [524288, 512], P(('replica', 'table')), may hold values from -45 to 45
- w_first: bfloat16 [512, 512], replicated, may hold values from -0.25 to 0.25
- w_second: bfloat16 [512, 512], replicated, may hold values from -0.25 to 0.25
Outputs:
- new_table: float32 [32768, 128], P('table')
- new_state: float32 [32768], P('table')
- new_first: bfloat16 [512, 512], replicated
- new_second: bfloat16 [512, 512], replicated
The draws below stay inside these ranges and needn't reach their ends.
Inputs may be any that keep to these rules, and one draw needn't show every extreme that they name: `block_ids`: within one device's 4 entries the block ids are distinct; entries of slots that are not live are not used. `block_counts`: some device uses all 4 slots in every draw.
All inputs are finite; a program needn't handle non-finite values.
Results may differ from the reference program's by a relative error of at most 0.00065.
The reference program's roundings to bfloat16 on the way (of `slot_grad`, `hidden` and `d_pre`) count: a program that leaves them out, or rounds other values in their place, can miss the bound.
Values may be sent and summed in bfloat16 or wider, within the bound.
A program may use at most 64 MiB of HBM per device.

```python
import math
import jax
import jax.numpy as jnp
from jax import lax

EMB = 128
HID = 512
BLOCK_ROWS = 128
SLOTS = 4
BLOCKS_DEV = 8
LOOK_DEV = 1024
ROWS_DEV = 1024
TABLE_ROWS = 32768
ROWS = 524288
N_REPLICA = 16
N_TABLE = 32


def draw_block_ids(key, part):
    keys = jax.random.split(key, N_REPLICA * N_TABLE)

    def choose(sub_key):
        return jax.random.permutation(sub_key, BLOCKS_DEV)[:SLOTS]
    chosen = jax.vmap(choose)(keys)
    return chosen.astype(jnp.int32).reshape(N_REPLICA, N_TABLE * SLOTS)


def draw_block_counts(key, part):
    first_key, second_key = jax.random.split(jax.random.fold_in(key, 11))
    counts = jax.random.randint(first_key, (N_REPLICA * N_TABLE,), 1, SLOTS + 1)
    full_at = jax.random.randint(second_key, (), 0, N_REPLICA * N_TABLE)
    counts = counts.at[full_at].set(SLOTS)
    return counts.astype(jnp.int32).reshape(N_REPLICA, N_TABLE)


def scaled_rows(key, factor):
    keys = jax.random.split(key, 3)
    base = jax.random.normal(keys[0], (ROWS, HID), jnp.float32)
    base = jnp.clip(base, -5.0, 5.0)
    row_scale = jnp.exp(jax.random.uniform(keys[1], (ROWS, 1), jnp.float32, math.log(0.3), math.log(3.0)))
    col_scale = jnp.exp(jax.random.uniform(keys[2], (1, HID), jnp.float32, math.log(0.3), math.log(3.0)))
    return factor * base * row_scale * col_scale


def draw_inputs(key, part):
    values = scaled_rows(jax.random.fold_in(key, 21), 1.0)
    device_of_row = jnp.arange(ROWS, dtype=jnp.int32) // ROWS_DEV
    spike_col = device_of_row % HID
    heavy = (spike_col[:, None] == jnp.arange(HID, dtype=jnp.int32)[None, :]).astype(jnp.float32)
    boost = 2.0 * math.sqrt(min(N_REPLICA * N_TABLE, HID))
    return (values * (1.0 + (boost - 1.0) * heavy)).astype(jnp.bfloat16)


def draw_cotangent(key, part):
    factor = (LOOK_DEV * EMB / (HID * HID * ROWS_DEV)) ** 0.5 / 6.0
    return scaled_rows(jax.random.fold_in(key, 37), factor).astype(jnp.bfloat16)


def plant(drawn, stream_key, smallest, top_value):
    index_at = [jax.random.randint(jax.random.fold_in(stream_key, axis), (), 0, length) for axis, length in enumerate(drawn.shape)]
    main_axis = drawn.shape.index(max(drawn.shape))
    neighbour = index_at[:main_axis] + [(index_at[main_axis] + 1) % drawn.shape[main_axis]] + index_at[main_axis + 1:]
    return drawn.at[tuple(index_at)].set(smallest).at[tuple(neighbour)].set(top_value)


def block_scale(own_key, dims, cuts, least, high):
    def one(position, parts):
        draws = jax.random.uniform(jax.random.fold_in(jax.random.fold_in(own_key, 6), position), (parts,), jnp.float32, least / len(cuts), high / len(cuts))
        return jnp.repeat(jnp.exp(draws), dims[position] // parts).reshape((-1,) + (1,) * (len(dims) - position - 1))

    gain = one(*cuts[0])
    for cut in cuts[1:]:
        gain = gain * one(*cut)
    return gain


def scatter_about(own_key, shape, spread, reach, cuts=(), kind=jnp.bfloat16):
    drawn = spread * jax.random.normal(own_key, shape, jnp.float32)
    if cuts:
        drawn = drawn * block_scale(own_key, shape, cuts, -0.22, 0.18)
    return jnp.clip(drawn, -reach, reach).astype(kind)


def setup_inputs(seed: int = 0) -> dict:
    key_of = jax.random.split(jax.random.key(seed), 12)
    table = scatter_about(key_of[0], (TABLE_ROWS, EMB), 0.1, 0.6, ((0, 32),), jnp.float32)
    row_state = jnp.clip(jnp.exp(math.log(2.384185791015625e-07) - 2.9957323 * jax.random.uniform(key_of[1], (TABLE_ROWS,), jnp.float32) ** block_scale(key_of[1], (TABLE_ROWS,), ((0, 32),), -0.2, 0.2)), 1.1920929132713809e-08, 2.384185791015625e-07)
    lookup_grads = scatter_about(key_of[2], (N_REPLICA, N_TABLE * LOOK_DEV, EMB), 1.0, 6.0, ((0, 16), (1, 32)))
    lookup_slots = plant(jax.random.randint(key_of[3], (N_REPLICA, N_TABLE * LOOK_DEV), 0, SLOTS), jax.random.fold_in(key_of[3], 1), 0, SLOTS - 1).astype(jnp.int32)
    lookup_rows = plant(jax.random.randint(key_of[4], (N_REPLICA, N_TABLE * LOOK_DEV), 0, BLOCK_ROWS), jax.random.fold_in(key_of[4], 1), 0, BLOCK_ROWS - 1).astype(jnp.int32)
    block_ids = draw_block_ids(jax.random.fold_in(key_of[11], 71), 0)
    block_counts = draw_block_counts(jax.random.fold_in(key_of[11], 71), 0)
    inputs = draw_inputs(jax.random.fold_in(key_of[11], 71), 0)
    cotangent = draw_cotangent(jax.random.fold_in(key_of[11], 71), 0)
    w_first = scatter_about(key_of[9], (HID, HID), HID ** -0.5, 0.25)
    w_second = scatter_about(key_of[10], (HID, HID), HID ** -0.5, 0.25)
    return {"table": table, "row_state": row_state, "lookup_grads": lookup_grads, "lookup_slots": lookup_slots, "lookup_rows": lookup_rows, "block_ids": block_ids, "block_counts": block_counts, "inputs": inputs, "cotangent": cotangent, "w_first": w_first, "w_second": w_second}


def mlp_terms(inputs, cotangent, w_first, w_second):
    pre = jnp.dot(inputs, w_first, preferred_element_type=jnp.float32)
    sig = jax.nn.sigmoid(pre)
    hidden = (pre * sig).astype(jnp.bfloat16)
    back = jnp.dot(cotangent, w_second.T, preferred_element_type=jnp.float32)
    d_pre = (back * sig * (1.0 + pre * (1.0 - sig))).astype(jnp.bfloat16)
    grad_first = jnp.dot(inputs.T, d_pre, preferred_element_type=jnp.float32)
    grad_second = jnp.dot(hidden.T, cotangent, preferred_element_type=jnp.float32)
    return (grad_first, grad_second)

def reference(table, row_state, lookup_grads, lookup_slots, lookup_rows, block_ids, block_counts, inputs, cotangent, w_first, w_second):
    reps = N_REPLICA
    tabs = N_TABLE
    slot_ids = lookup_slots.reshape(reps, tabs, LOOK_DEV)
    row_ids = lookup_rows.reshape(reps, tabs, LOOK_DEV)
    live_look = (slot_ids < block_counts[:, :, None]).astype(jnp.float32)
    device_ids = (jnp.arange(reps, dtype=jnp.int32)[:, None] * tabs + jnp.arange(tabs, dtype=jnp.int32)[None, :]).astype(jnp.int32)
    flat_ids = ((device_ids[:, :, None] * SLOTS + slot_ids) * BLOCK_ROWS + row_ids).astype(jnp.int32).reshape(-1)
    grad_rows = lookup_grads.reshape(-1, EMB).astype(jnp.float32) * live_look.reshape(-1, 1)
    slot_grad = jax.ops.segment_sum(grad_rows, flat_ids, num_segments=reps * tabs * SLOTS * BLOCK_ROWS).astype(jnp.bfloat16)
    ids = block_ids.reshape(reps, tabs, SLOTS)
    live_slot = (jnp.arange(SLOTS, dtype=jnp.int32)[None, None, :] < block_counts[:, :, None]).astype(jnp.float32)
    dest_block = (jnp.arange(tabs, dtype=jnp.int32)[None, :, None] * BLOCKS_DEV + ids).astype(jnp.int32)
    dest = (dest_block[..., None] * BLOCK_ROWS + jnp.arange(BLOCK_ROWS, dtype=jnp.int32)).astype(jnp.int32).reshape(-1)
    weights = jnp.broadcast_to(live_slot[..., None], (reps, tabs, SLOTS, BLOCK_ROWS)).reshape(-1, 1)
    merged = jax.ops.segment_sum(slot_grad.astype(jnp.float32) * weights, dest, num_segments=tabs * BLOCKS_DEV * BLOCK_ROWS)
    xs = inputs.reshape(-1, ROWS_DEV, HID)
    ys = cotangent.reshape(-1, ROWS_DEV, HID)

    def step(carry, pair):
        first, second = mlp_terms(pair[0], pair[1], w_first, w_second)
        return ((carry[0] + first, carry[1] + second), None)
    zeros = jnp.zeros((HID, HID), jnp.float32)
    (grad_first, grad_second), _ = lax.scan(step, (zeros, zeros), (xs, ys))
    total = jnp.sum(merged * merged) + jnp.sum(grad_first * grad_first) + jnp.sum(grad_second * grad_second)
    clip_scale = jnp.minimum(1.0, 1.0 / (jnp.sqrt(total) + 1e-06))
    clipped = clip_scale * merged
    new_state = row_state + lax.optimization_barrier(jnp.mean(clipped * clipped, axis=1))
    new_table = table - 0.05 * clipped / jnp.sqrt(new_state)[:, None]
    rate = 0.04 * HID
    new_first = (w_first.astype(jnp.float32) - rate * clip_scale * grad_first).astype(jnp.bfloat16)
    new_second = (w_second.astype(jnp.float32) - rate * clip_scale * grad_second).astype(jnp.bfloat16)
    return (new_table, new_state, new_first, new_second)
```

```python
import jax
import jax.numpy as jnp
from jax import lax
from jax.experimental import pallas as pl
from jax.experimental.pallas import tpu as pltpu
from jax.sharding import PartitionSpec as P

X, Y, Z, C = 4, 8, 8, 2
BLOCK_ROWS = 128
EMB = 128
HID = 512
SLOTS = 4
BLOCKS = 8
SAMPLES = 1024
LOOKUPS = 1024
ROWS = BLOCKS * BLOCK_ROWS
SHARE = ROWS // (Z * C)
CHUNK = 256

EMB_RATE = 0.05
MLP_RATE = 0.04 * HID
F32 = jnp.float32
BF16 = jnp.bfloat16
MESH = pl.DeviceIdType.MESH


def kernel(
    table_hbm, state_ref, grads_hbm, slots_ref, rows_ref, ids_ref, count_ref,
    inputs_hbm, cot_hbm, w1_hbm, w2_hbm,
    new_table, new_state, new_first, new_second,
    table, lgrads, w1, w2, left, right,
    dense, emb_recv, merged,
    g_sib, g_own, g_recv,
    r1x, r1y, r1z, t2y, t2z, r2y, r2z, r3x, r3y, r3z, w4y, w4z, f5x, f5y, f5z,
    in_sem, send_sem, recv_sem,
):
    rep = lax.axis_index("replica")
    tab = lax.axis_index("table")
    z, c = rep // C, lax.rem(rep, C)
    x, y = tab // Y, lax.rem(tab, Y)
    sib = 1 - c

    def at_x(d):
        return (rep, lax.rem(x + d, X) * Y + y)

    def at_y(d):
        return (rep, x * Y + lax.rem(y + d, Y))

    def at_z(d, core=c):
        return (lax.rem(z + d, Z) * C + core, tab)

    sibling = (z * C + sib, tab)

    def send(src, dst, k, dev):
        pltpu.make_async_remote_copy(
            src_ref=src, dst_ref=dst, send_sem=send_sem.at[k], recv_sem=recv_sem.at[k],
            device_id=dev, device_id_type=MESH,
        ).start()

    def take(ref, k):
        pltpu.make_async_copy(ref, ref, recv_sem.at[k]).wait()

    def sent(ref, k):
        pltpu.make_async_copy(ref, ref, send_sem.at[k]).wait()

    loads = [
        pltpu.make_async_copy(grads_hbm.at[0], lgrads, in_sem.at[0]),
        pltpu.make_async_copy(w1_hbm, w1, in_sem.at[1]),
        pltpu.make_async_copy(inputs_hbm, left.at[0], in_sem.at[2]),
        pltpu.make_async_copy(w2_hbm, w2, in_sem.at[3]),
        pltpu.make_async_copy(cot_hbm, right.at[1], in_sem.at[4]),
        pltpu.make_async_copy(table_hbm, table, in_sem.at[5]),
    ]
    for load in loads:
        load.start()

    barrier = pltpu.get_barrier_semaphore()
    peers = [at_x(d) for d in range(1, X)] + [at_y(d) for d in range(1, Y)]
    peers += [at_z(d) for d in range(1, Z)] + [at_z(d, sib) for d in range(Z)]
    for dev in peers:
        pl.semaphore_signal(barrier, inc=1, device_id=dev, device_id_type=MESH)

    count = count_ref[0, 0]
    slot_ids = slots_ref[...]
    position = jnp.where(slot_ids < count, slot_ids * BLOCK_ROWS + rows_ref[...], -1)
    loads[0].wait()
    lookup_grads = lgrads[...]
    slot_sums = []
    for k in range(SLOTS):
        target = lax.broadcasted_iota(jnp.int32, (BLOCK_ROWS, LOOKUPS), 0) + k * BLOCK_ROWS
        onehot = jnp.where(target == position, 1.0, 0.0).astype(BF16)
        summed = jnp.dot(onehot, lookup_grads, preferred_element_type=F32)
        slot_sums.append(summed.astype(BF16).astype(F32))
    for b in range(BLOCKS):
        block = jnp.zeros((BLOCK_ROWS, EMB), F32)
        for k in range(SLOTS):
            block += jnp.where((ids_ref[0, k] == b) & (k < count), 1.0, 0.0) * slot_sums[k]
        dense[pl.ds(b * BLOCK_ROWS, BLOCK_ROWS)] = block.astype(BF16)

    def share(zz, cc):
        return pl.ds(pl.multiple_of((cc * Z + zz) * SHARE, SHARE), SHARE)

    pl.semaphore_wait(barrier, len(peers))
    for d in range(Z):
        for same in (True, False):
            if d == 0 and same:
                continue
            core = c if same else sib
            send(dense.at[share(lax.rem(z + d, Z), core)], emb_recv.at[rep], 0, at_z(d, core))
    emb_recv[rep] = dense[share(z, c)]

    for load in loads[1:5]:
        load.wait()

    def mlp(i, _):
        rows = pl.ds(pl.multiple_of(i * CHUNK, CHUNK), CHUNK)
        pre = jnp.dot(left[0, rows], w1[...], preferred_element_type=F32)
        sig = jax.nn.sigmoid(pre)
        left[1, rows] = (pre * sig).astype(BF16)
        back = lax.dot_general(
            right[1, rows], w2[...], (((1,), (1,)), ((), ())), preferred_element_type=F32
        )
        right[0, rows] = (back * sig * (1.0 + pre * (1.0 - sig))).astype(BF16)
        return 0

    lax.fori_loop(0, SAMPLES // CHUNK, mlp, 0)

    def grad(which, half):
        cols = pl.ds(pl.multiple_of(half * 256, 256), 256)
        return lax.dot_general(
            left[which], right[which, :, cols], (((0,), (0,)), ((), ())),
            preferred_element_type=F32,
        )

    for half in range(2):
        g = grad(sib, half)
        g_sib[2 * half] = g[:, :128]
        g_sib[2 * half + 1] = g[:, 128:]
        send(g_sib.at[pl.ds(2 * half, 2)], g_recv.at[pl.ds(2 * half, 2)], 1 + half, sibling)

    take(emb_recv.at[pl.ds(0, Z * C - 1)], 0)
    total = emb_recv[0].astype(F32)
    for k in range(1, Z * C):
        total += emb_recv[k].astype(F32)
    merged[share(z, c)] = total
    for d in range(1, Z):
        send(merged.at[share(z, c)], merged.at[share(z, c)], 3, at_z(d))

    for half in range(2):
        g = grad(c, half)
        g_own[2 * half] = g[:, :128]
        g_own[2 * half + 1] = g[:, 128:]

    take(g_recv.at[pl.ds(0, 2)], 1)
    g_own[0:2] = g_own[0:2] + g_recv[0:2]
    for d in range(1, X):
        rows = pl.ds(pl.multiple_of(lax.rem(x + d, X) * 128, 128), 128)
        send(g_own.at[pl.ds(0, 2), rows], r1x.at[d - 1], 4, at_x(d))
    take(g_recv.at[pl.ds(2, 2)], 2)
    g_own[2:4] = g_own[2:4] + g_recv[2:4]
    for d in range(1, Y):
        rows = pl.ds(pl.multiple_of(lax.rem(y + d, Y) * 64, 64), 64)
        send(g_own.at[2, rows], r1y.at[d - 1], 5, at_y(d))
        rows = pl.ds(pl.multiple_of(lax.rem(z + d, Z) * 64, 64), 64)
        send(g_own.at[3, rows], r1z.at[d - 1], 6, at_z(d))

    half_rows = pl.ds(pl.multiple_of(c * (ROWS // 2), ROWS // 2), ROWS // 2)
    take(merged.at[pl.ds(0, SHARE * (Z - 1))], 3)
    send(merged.at[half_rows], merged.at[half_rows], 7, sibling)

    def summed(ref, n, first):
        for k in range(n):
            first = first + ref[k]
        return first

    take(r1x, 4)
    own = pl.ds(pl.multiple_of(x * 128, 128), 128)
    s = summed(r1x, X - 1, g_own[0:2, own])
    t2y[:, 0:16] = s[0].reshape(Y, 16, 128)
    t2z[:, 0:16] = s[1].reshape(Z, 16, 128)
    take(r1y, 5)
    s = summed(r1y, Y - 1, g_own[2, pl.ds(pl.multiple_of(y * 64, 64), 64)])
    t2z[:, 16:24] = s.reshape(Z, 8, 128)
    for d in range(1, Z):
        send(t2z.at[lax.rem(z + d, Z)], r2z.at[d - 1], 8, at_z(d))
    take(r1z, 6)
    s = summed(r1z, Z - 1, g_own[3, pl.ds(pl.multiple_of(z * 64, 64), 64)])
    t2y[:, 16:24] = s.reshape(Y, 8, 128)
    for d in range(1, Y):
        send(t2y.at[lax.rem(y + d, Y)], r2y.at[d - 1], 9, at_y(d))

    take(merged.at[half_rows], 7)
    lane = lax.broadcasted_iota(jnp.int32, (BLOCK_ROWS, 128), 1)
    squares = jnp.zeros((BLOCK_ROWS, 128), F32)
    for b in range(BLOCKS):
        m = merged[pl.ds(b * BLOCK_ROWS, BLOCK_ROWS)]
        squares = jnp.where(lane == b, jnp.sum(m * m, axis=1, keepdims=True), squares)
    emb_part = jnp.sum(squares)
    squares = squares * (1.0 / EMB)
    squares_row = jnp.transpose(squares)[0:BLOCKS]
    state_row = state_ref[...]
    state_col = jnp.transpose(
        jnp.concatenate([state_row, jnp.zeros((BLOCK_ROWS - BLOCKS, 128), F32)], axis=0)
    )

    take(r2z, 8)
    s_z = summed(r2z, Z - 1, t2z[z])
    r3y[y] = s_z[0:16]
    for d in range(1, Y):
        send(r3y.at[y], r3y.at[y], 10, at_y(d))
    take(r2y, 9)
    s_y = summed(r2y, Y - 1, t2y[y])
    r3z[z] = s_y[0:16]
    for d in range(1, Z):
        send(r3z.at[z], r3z.at[z], 11, at_z(d))
    r3x[x, 0:8] = s_y[16:24]
    r3x[x, 8:16] = s_z[16:24]
    for d in range(1, X):
        send(r3x.at[x], r3x.at[x], 12, at_x(d))

    take(r3x.at[pl.ds(0, X - 1)], 12)
    both = summed(r3x, X, 0.0)
    w4y[y, 16:24] = both[0:8]
    w4z[z, 16:24] = both[8:16]
    w4y[y, 24:32] = jnp.full((8, 128), emb_part, F32)
    take(r3y.at[pl.ds(0, Y - 1)], 10)
    w4z[z, 0:16] = summed(r3y, Y, 0.0)
    for d in range(1, Z):
        send(w4z.at[z], w4z.at[z], 13, at_z(d))
    take(r3z.at[pl.ds(0, Z - 1)], 11)
    w4y[y, 0:16] = summed(r3z, Z, 0.0)
    for d in range(1, Y):
        send(w4y.at[y], w4y.at[y], 14, at_y(d))

    take(w4z.at[pl.ds(0, Z - 1)], 13)
    f5y[c, y] = w4z[:, 16:24].reshape(64, 128)
    for d in range(1, Y):
        send(f5y.at[c, y], f5y.at[c, y], 15, at_y(d))
    f5x[c, x, 128:256] = w4z[:, 0:16].reshape(128, 128)
    take(w4y.at[pl.ds(0, Y - 1)], 14)
    f5x[c, x, 0:128] = w4y[:, 0:16].reshape(128, 128)
    f5x[c, x, 256:264] = jnp.sum(w4y[:, 24:32], axis=0)
    for d in range(1, X):
        send(f5x.at[c, x], f5x.at[c, x], 16, at_x(d))
    f5z[c, z] = w4y[:, 16:24].reshape(64, 128)
    for d in range(1, Z):
        send(f5z.at[c, z], f5z.at[c, z], 17, at_z(d))

    take(f5y.at[0, pl.ds(0, Y - 1)], 15)
    send(f5y.at[c], f5y.at[c], 18, sibling)
    take(f5x.at[0, pl.ds(0, X - 1)], 16)
    send(f5x.at[c], f5x.at[c], 19, sibling)
    take(f5z.at[0, pl.ds(0, Z - 1)], 17)
    send(f5z.at[c], f5z.at[c], 20, sibling)
    loads[5].wait()
    take(f5y.at[0], 18)
    take(f5x.at[0], 19)
    take(f5z.at[0], 20)

    squared = jnp.zeros((64, 128), F32)
    for core in range(C):
        for k in range(Y):
            v = f5y[core, k]
            squared += v * v
            v = f5z[core, k]
            squared += v * v
        for k in range(X):
            for q in range(4):
                v = f5x[core, k, 64 * q:64 * q + 64]
                squared += v * v
    emb_total = f5x[0, 0, 256:257, 0:1]
    for k in range(1, X):
        emb_total = emb_total + f5x[0, k, 256:257, 0:1]
    total = jnp.sum(squared, keepdims=True) + emb_total
    clip = jnp.minimum(1.0, 1.0 / (jnp.sqrt(total) + 1e-06))

    rate = MLP_RATE * clip
    for core, (w, out) in enumerate(((w1, new_first), (w2, new_second))):
        for q in range(2):
            cols = pl.ds(128 * q, 128)
            for k in range(X):
                rows = pl.ds(128 * k, 128)
                g = f5x[core, k, 128 * q:128 * q + 128]
                out[rows, cols] = (w[rows, cols].astype(F32) - rate * g).astype(BF16)
        for q, ref in ((2, f5y), (3, f5z)):
            cols = pl.ds(128 * q, 128)
            g = ref[core].reshape(HID, 128)
            out[:, cols] = (w[:, cols].astype(F32) - rate * g).astype(BF16)
    clip_sq = clip * clip
    new_state[...] = state_row + clip_sq * squares_row
    scale = (EMB_RATE * clip) / jnp.sqrt(state_col + clip_sq * squares)
    for b in range(BLOCKS):
        rows = pl.ds(b * BLOCK_ROWS, BLOCK_ROWS)
        new_table[rows] = table[rows] - merged[rows] * scale[:, b:b + 1]

    sent(emb_recv.at[pl.ds(0, Z * C - 1)], 0)
    sent(g_recv.at[pl.ds(0, 2)], 1)
    sent(g_recv.at[pl.ds(2, 2)], 2)
    sent(merged.at[pl.ds(0, SHARE * (Z - 1))], 3)
    sent(r1x, 4)
    sent(r1y, 5)
    sent(r1z, 6)
    sent(merged.at[half_rows], 7)
    sent(r2z, 8)
    sent(r2y, 9)
    sent(r3y.at[pl.ds(0, Y - 1)], 10)
    sent(r3z.at[pl.ds(0, Z - 1)], 11)
    sent(r3x.at[pl.ds(0, X - 1)], 12)
    sent(w4z.at[pl.ds(0, Z - 1)], 13)
    sent(w4y.at[pl.ds(0, Y - 1)], 14)
    sent(f5y.at[0, pl.ds(0, Y - 1)], 15)
    sent(f5x.at[0, pl.ds(0, X - 1)], 16)
    sent(f5z.at[0, pl.ds(0, Z - 1)], 17)
    sent(f5y.at[0], 18)
    sent(f5x.at[0], 19)
    sent(f5z.at[0], 20)


def on_device(
    table, row_state, lookup_grads, lookup_slots, lookup_rows, block_ids, block_counts,
    inputs, cotangent, w_first, w_second,
):
    vmem = pl.BlockSpec(memory_space=pltpu.VMEM)
    smem = pl.BlockSpec(memory_space=pltpu.SMEM)
    hbm = pl.BlockSpec(memory_space=pl.ANY)
    new_table, new_state, new_first, new_second = pl.pallas_call(
        kernel,
        out_shape=(
            jax.ShapeDtypeStruct((ROWS, EMB), F32),
            jax.ShapeDtypeStruct((BLOCKS, BLOCK_ROWS), F32),
            jax.ShapeDtypeStruct((HID, HID), BF16),
            jax.ShapeDtypeStruct((HID, HID), BF16),
        ),
        in_specs=[hbm, vmem, hbm, vmem, vmem, smem, smem, hbm, hbm, hbm, hbm],
        out_specs=(vmem, vmem, vmem, vmem),
        scratch_shapes=[
            pltpu.VMEM((ROWS, EMB), F32),
            pltpu.VMEM((LOOKUPS, EMB), BF16),
            pltpu.VMEM((HID, HID), BF16),
            pltpu.VMEM((HID, HID), BF16),
            pltpu.VMEM((2, SAMPLES, HID), BF16),
            pltpu.VMEM((2, SAMPLES, HID), BF16),
            pltpu.VMEM((ROWS, EMB), BF16),
            pltpu.VMEM((Z * C, SHARE, EMB), BF16),
            pltpu.VMEM((ROWS, EMB), F32),
            pltpu.VMEM((4, HID, 128), F32),
            pltpu.VMEM((4, HID, 128), F32),
            pltpu.VMEM((4, HID, 128), F32),
            pltpu.VMEM((X - 1, 2, 128, 128), F32),
            pltpu.VMEM((Y - 1, 64, 128), F32),
            pltpu.VMEM((Z - 1, 64, 128), F32),
            pltpu.VMEM((Y, 24, 128), F32),
            pltpu.VMEM((Z, 24, 128), F32),
            pltpu.VMEM((Y - 1, 24, 128), F32),
            pltpu.VMEM((Z - 1, 24, 128), F32),
            pltpu.VMEM((X, 16, 128), F32),
            pltpu.VMEM((Y, 16, 128), F32),
            pltpu.VMEM((Z, 16, 128), F32),
            pltpu.VMEM((Y, 32, 128), F32),
            pltpu.VMEM((Z, 24, 128), F32),
            pltpu.VMEM((C, X, 264, 128), F32),
            pltpu.VMEM((C, Y, 64, 128), F32),
            pltpu.VMEM((C, Z, 64, 128), F32),
            pltpu.SemaphoreType.DMA((6,)),
            pltpu.SemaphoreType.DMA((21,)),
            pltpu.SemaphoreType.DMA((21,)),
        ],
        compiler_params=pltpu.CompilerParams(
            collective_id=0, has_side_effects=True, vmem_limit_bytes=48 * 2**20
        ),
        cost_estimate=pl.CostEstimate(
            flops=2_400_000_000, bytes_accessed=6 * 2**20, transcendentals=2**20
        ),
        name="step",
    )(
        table, row_state.reshape(BLOCKS, BLOCK_ROWS), lookup_grads, lookup_slots, lookup_rows,
        block_ids, block_counts, inputs, cotangent, w_first, w_second,
    )
    return (new_table, new_state.reshape(ROWS), new_first, new_second)


def solution(mesh):
    placed = (
        P("table", None),
        P("table"),
        P("replica", "table", None),
        P("replica", "table"),
        P("replica", "table"),
        P("replica", "table"),
        P("replica", "table"),
        P(("replica", "table"), None),
        P(("replica", "table"), None),
        P(),
        P(),
    )
    return jax.shard_map(
        on_device,
        mesh=mesh,
        in_specs=placed,
        out_specs=(P("table", None), P("table"), P(), P()),
        check_vma=False,
    )
```

```python
import jax
import jax.numpy as jnp
from jax import lax
from jax.experimental import pallas as pl
from jax.experimental.pallas import tpu as pltpu
from jax.sharding import PartitionSpec as P

X, Y, Z, C = 4, 8, 8, 2
BLOCK_ROWS = 128
EMB = 128
HID = 512
SLOTS = 4
BLOCKS = 8
SAMPLES = 1024
LOOKUPS = 1024
ROWS = BLOCKS * BLOCK_ROWS
SHARE = ROWS // (Z * C)
CHUNK = 256
FAR = {4: (2, 1, 3), 8: (4, 3, 5, 2, 6, 1, 7)}

EMB_RATE = 0.05
MLP_RATE = 0.04 * HID
F32 = jnp.float32
BF16 = jnp.bfloat16
MESH = pl.DeviceIdType.MESH


def kernel(
    table_hbm, state_hbm, grads_hbm, slots_hbm, rows_hbm, ids_hbm, count_hbm,
    inputs_hbm, cot_hbm, w1_hbm, w2_hbm,
    new_table, new_state, new_first, new_second,
    table, state_ref, lgrads, slots_ref, rows_ref, ids_ref, count_ref, w1, w2, left, right,
    dense, emb_recv, merged,
    g_sib, g_own, g_recv,
    r1x, r1y, r1z, t2y, t2z, r2y, r2z, r3x, r3y, r3z, w4y, w4z, f5x, f5y, f5z,
    in_sem, out_sem, send_sem, recv_sem,
):
    rep = lax.axis_index("replica")
    tab = lax.axis_index("table")
    z, c = rep // C, lax.rem(rep, C)
    x, y = tab // Y, lax.rem(tab, Y)
    sib = 1 - c

    def at_x(d):
        return (rep, lax.rem(x + d, X) * Y + y)

    def at_y(d):
        return (rep, x * Y + lax.rem(y + d, Y))

    def at_z(d, core=c):
        return (lax.rem(z + d, Z) * C + core, tab)

    sibling = (z * C + sib, tab)

    opened, taken = {}, set()

    def send(src, dst, k, dev, whole):
        opened[k] = whole
        pltpu.make_async_remote_copy(
            src_ref=src, dst_ref=dst, send_sem=send_sem.at[k], recv_sem=recv_sem.at[k],
            device_id=dev, device_id_type=MESH,
        ).start()

    def take(k):
        taken.add(k)
        pltpu.make_async_copy(opened[k], opened[k], recv_sem.at[k]).wait()

    def finish():
        for k, whole in opened.items():
            if k not in taken:
                take(k)
            pltpu.make_async_copy(whole, whole, send_sem.at[k]).wait()

    parts = [pl.ds(k * CHUNK, CHUNK) for k in range(SAMPLES // CHUNK)]
    pairs = [
        (count_hbm, count_ref), (ids_hbm, ids_ref), (slots_hbm, slots_ref), (rows_hbm, rows_ref),
        (grads_hbm.at[0], lgrads), (w1_hbm, w1), (w2_hbm, w2),
    ]
    for rows in parts:
        pairs += [(inputs_hbm.at[rows], left.at[0, rows]), (cot_hbm.at[rows], right.at[1, rows])]
    pairs += [(state_hbm, state_ref), (table_hbm, table)]
    loads = [pltpu.make_async_copy(*pair, in_sem.at[k]) for k, pair in enumerate(pairs)]
    for load in loads:
        load.start()

    barrier = pltpu.get_barrier_semaphore()
    peers = [at_x(d) for d in range(1, X)] + [at_y(d) for d in range(1, Y)]
    peers += [at_z(d) for d in range(1, Z)] + [at_z(d, sib) for d in range(Z)]
    for dev in peers:
        pl.semaphore_signal(barrier, inc=1, device_id=dev, device_id_type=MESH)

    for load in loads[:5]:
        load.wait()
    count = count_ref[0, 0]
    slot_ids = slots_ref[...]
    position = jnp.where(slot_ids < count, slot_ids * BLOCK_ROWS + rows_ref[...], -1)
    lookup_grads = lgrads[...]
    slot_sums = []
    for k in range(SLOTS):
        target = lax.broadcasted_iota(jnp.int32, (BLOCK_ROWS, LOOKUPS), 0) + k * BLOCK_ROWS
        onehot = jnp.where(target == position, 1.0, 0.0).astype(BF16)
        summed = jnp.dot(onehot, lookup_grads, preferred_element_type=F32)
        slot_sums.append(summed.astype(BF16).astype(F32))
    for b in range(BLOCKS):
        block = jnp.zeros((BLOCK_ROWS, EMB), F32)
        for k in range(SLOTS):
            block += jnp.where((ids_ref[0, k] == b) & (k < count), 1.0, 0.0) * slot_sums[k]
        dense[pl.ds(b * BLOCK_ROWS, BLOCK_ROWS)] = block.astype(BF16)

    def share(zz, cc):
        return pl.ds(pl.multiple_of((cc * Z + zz) * SHARE, SHARE), SHARE)

    loads[5].wait()
    loads[6].wait()
    for k, rows in enumerate(parts):
        loads[7 + 2 * k].wait()
        loads[8 + 2 * k].wait()
        pre = jnp.dot(left[0, rows], w1[...], preferred_element_type=F32)
        back = lax.dot_general(
            right[1, rows], w2[...], (((1,), (1,)), ((), ())), preferred_element_type=F32
        )
        sig = jax.nn.sigmoid(pre)
        left[1, rows] = (pre * sig).astype(BF16)
        right[0, rows] = (back * sig * (1.0 + pre * (1.0 - sig))).astype(BF16)

    def grad(which, half):
        cols = pl.ds(half * 256, 256)
        return lax.dot_general(
            left[which], right[which, :, cols], (((0,), (0,)), ((), ())),
            preferred_element_type=F32,
        )

    pl.semaphore_wait(barrier, len(peers))
    for half in (1, 0):
        g = grad(sib, half)
        g_sib[2 * half] = g[:, :128]
        g_sib[2 * half + 1] = g[:, 128:]
        two = pl.ds(2 * half, 2)
        send(g_sib.at[two], g_recv.at[two], 1 + half, sibling, g_recv.at[two])
    for half in (1, 0):
        g = grad(c, half)
        g_own[2 * half] = g[:, :128]
        g_own[2 * half + 1] = g[:, 128:]

    for d in FAR[Z] + (0,):
        for core in (c, sib):
            if d == 0 and core is c:
                continue
            send(
                dense.at[share(lax.rem(z + d, Z), core)], emb_recv.at[rep], 0, at_z(d, core),
                emb_recv.at[pl.ds(0, Z * C - 1)],
            )
    emb_recv[rep] = dense[share(z, c)]

    take(2)
    g_own[2:4] = g_own[2:4] + g_recv[2:4]
    for d in FAR[Y]:
        rows = pl.ds(pl.multiple_of(lax.rem(y + d, Y) * 64, 64), 64)
        send(g_own.at[2, rows], r1y.at[d - 1], 5, at_y(d), r1y)
        rows = pl.ds(pl.multiple_of(lax.rem(z + d, Z) * 64, 64), 64)
        send(g_own.at[3, rows], r1z.at[d - 1], 6, at_z(d), r1z)
    take(1)
    g_own[0:2] = g_own[0:2] + g_recv[0:2]
    for d in FAR[X]:
        rows = pl.ds(pl.multiple_of(lax.rem(x + d, X) * 128, 128), 128)
        send(g_own.at[pl.ds(0, 2), rows], r1x.at[d - 1], 4, at_x(d), r1x)

    def summed(ref, n, first):
        for k in range(n):
            first = first + ref[k]
        return first

    take(4)
    own = pl.ds(pl.multiple_of(x * 128, 128), 128)
    s = summed(r1x, X - 1, g_own[0:2, own])
    t2y[:, 0:16] = s[0].reshape(Y, 16, 128)
    t2z[:, 0:16] = s[1].reshape(Z, 16, 128)
    take(5)
    s = summed(r1y, Y - 1, g_own[2, pl.ds(pl.multiple_of(y * 64, 64), 64)])
    t2z[:, 16:24] = s.reshape(Z, 8, 128)
    for d in FAR[Z]:
        send(t2z.at[lax.rem(z + d, Z)], r2z.at[d - 1], 8, at_z(d), r2z)
    take(6)
    s = summed(r1z, Z - 1, g_own[3, pl.ds(pl.multiple_of(z * 64, 64), 64)])
    t2y[:, 16:24] = s.reshape(Y, 8, 128)
    for d in FAR[Y]:
        send(t2y.at[lax.rem(y + d, Y)], r2y.at[d - 1], 9, at_y(d), r2y)

    take(0)
    total = emb_recv[0].astype(F32)
    for k in range(1, Z * C):
        total += emb_recv[k].astype(F32)
    merged[share(z, c)] = total
    for d in FAR[Z]:
        send(
            merged.at[share(z, c)], merged.at[share(z, c)], 3, at_z(d),
            merged.at[pl.ds(0, SHARE * (Z - 1))],
        )

    take(8)
    s_z = summed(r2z, Z - 1, t2z[z])
    r3y[y] = s_z[0:16]
    for d in FAR[Y]:
        send(r3y.at[y], r3y.at[y], 10, at_y(d), r3y.at[pl.ds(0, Y - 1)])
    take(9)
    s_y = summed(r2y, Y - 1, t2y[y])
    r3z[z] = s_y[0:16]
    for d in FAR[Z]:
        send(r3z.at[z], r3z.at[z], 11, at_z(d), r3z.at[pl.ds(0, Z - 1)])
    r3x[x, 0:8] = s_y[16:24]
    r3x[x, 8:16] = s_z[16:24]
    for d in FAR[X]:
        send(r3x.at[x], r3x.at[x], 12, at_x(d), r3x.at[pl.ds(0, X - 1)])

    half_rows = pl.ds(pl.multiple_of(c * (ROWS // 2), ROWS // 2), ROWS // 2)
    take(3)
    send(merged.at[half_rows], merged.at[half_rows], 7, sibling, merged.at[half_rows])
    lane = lax.broadcasted_iota(jnp.int32, (BLOCK_ROWS, 128), 1)

    def squares_of(core):
        found = jnp.zeros((BLOCK_ROWS, 128), F32)
        for k in range(BLOCKS // C):
            b = core * (BLOCKS // C) + k
            m = merged[pl.ds(pl.multiple_of(b * BLOCK_ROWS, BLOCK_ROWS), BLOCK_ROWS)]
            found = jnp.where(lane == b, jnp.sum(m * m, axis=1, keepdims=True), found)
        return found

    squares = squares_of(c)
    emb_part = jnp.sum(squares)

    take(12)
    both = summed(r3x, X, 0.0)
    w4y[y, 16:24] = both[0:8]
    w4z[z, 16:24] = both[8:16]
    w4y[y, 24:32] = jnp.full((8, 128), emb_part, F32)
    take(10)
    w4z[z, 0:16] = summed(r3y, Y, 0.0)
    for d in FAR[Z]:
        send(w4z.at[z], w4z.at[z], 13, at_z(d), w4z.at[pl.ds(0, Z - 1)])
    take(11)
    w4y[y, 0:16] = summed(r3z, Z, 0.0)
    for d in FAR[Y]:
        send(w4y.at[y], w4y.at[y], 14, at_y(d), w4y.at[pl.ds(0, Y - 1)])

    take(7)
    squares = (squares + squares_of(sib)) * (1.0 / EMB)
    squares_row = jnp.transpose(squares)[0:BLOCKS]
    loads[-2].wait()
    state_row = state_ref[...]
    state_col = jnp.transpose(
        jnp.concatenate([state_row, jnp.zeros((BLOCK_ROWS - BLOCKS, 128), F32)], axis=0)
    )

    take(13)
    f5y[c, y] = w4z[:, 16:24].reshape(64, 128)
    for d in FAR[Y]:
        send(f5y.at[c, y], f5y.at[c, y], 15, at_y(d), f5y.at[0, pl.ds(0, Y - 1)])
    f5x[c, x, 128:256] = w4z[:, 0:16].reshape(128, 128)
    take(14)
    f5z[c, z] = w4y[:, 16:24].reshape(64, 128)
    for d in FAR[Z]:
        send(f5z.at[c, z], f5z.at[c, z], 17, at_z(d), f5z.at[0, pl.ds(0, Z - 1)])
    f5x[c, x, 0:128] = w4y[:, 0:16].reshape(128, 128)
    f5x[c, x, 256:264] = jnp.sum(w4y[:, 24:32], axis=0)
    for d in FAR[X]:
        send(f5x.at[c, x], f5x.at[c, x], 16, at_x(d), f5x.at[0, pl.ds(0, X - 1)])

    def squared(core, ref, n, rows):
        found = jnp.zeros((64, 128), F32)
        for k in range(n):
            for q in range(rows // 64):
                v = ref[core, k, 64 * q:64 * q + 64]
                found += v * v
        return found

    def emb_of(core):
        found = f5x[core, 0, 256:264]
        for k in range(1, X):
            found = found + f5x[core, k, 256:264]
        return found[0:1, 0:1]

    take(15)
    send(f5y.at[c], f5y.at[c], 18, sibling, f5y.at[0])
    take(17)
    send(f5z.at[c], f5z.at[c], 20, sibling, f5z.at[0])
    take(16)
    send(f5x.at[c], f5x.at[c], 19, sibling, f5x.at[0])
    mine = squared(c, f5y, Y, 64) + squared(c, f5z, Z, 64) + squared(c, f5x, X, 256)
    loads[-1].wait()
    take(18)
    take(20)
    take(19)
    other = squared(sib, f5y, Y, 64) + squared(sib, f5z, Z, 64) + squared(sib, f5x, X, 256)

    total = jnp.sum(mine + other, keepdims=True) + (emb_of(c) + emb_of(sib))
    clip = jnp.minimum(1.0, 1.0 / (jnp.sqrt(total) + 1e-06))

    def store(src, dst, k):
        copy = pltpu.make_async_copy(src, dst, out_sem.at[k])
        copy.start()
        return copy

    clip_sq = clip * clip
    scale = (EMB_RATE * clip) / jnp.sqrt(state_col + clip_sq * squares)
    for b in range(BLOCKS):
        rows = pl.ds(b * BLOCK_ROWS, BLOCK_ROWS)
        table[rows] = table[rows] - merged[rows] * scale[:, b:b + 1]
    stores = [store(table, new_table, 0)]
    state_ref[...] = state_row + clip_sq * squares_row
    stores.append(store(state_ref, new_state, 1))
    rate = MLP_RATE * clip
    for core, (w, out) in enumerate(((w1, new_first), (w2, new_second))):
        for q in range(2):
            cols = pl.ds(128 * q, 128)
            for k in range(X):
                rows = pl.ds(128 * k, 128)
                g = f5x[core, k, 128 * q:128 * q + 128]
                w[rows, cols] = (w[rows, cols].astype(F32) - rate * g).astype(BF16)
        for q, ref in ((2, f5y), (3, f5z)):
            cols = pl.ds(128 * q, 128)
            g = ref[core].reshape(HID, 128)
            w[:, cols] = (w[:, cols].astype(F32) - rate * g).astype(BF16)
        stores.append(store(w, out, 2 + core))
    finish()
    for copy in stores:
        copy.wait()


def hand_over(*refs):
    n = len(refs) // 3
    arrays, held, sem = refs[: 2 * n], refs[2 * n : 3 * n], refs[-1]
    loads = [pltpu.make_async_copy(arrays[k], held[k], sem.at[k]) for k in range(n)]
    stores = [pltpu.make_async_copy(held[k], arrays[n + k], sem.at[n + k]) for k in range(n)]
    for load in loads:
        load.start()
    for load, store in zip(loads, stores):
        load.wait()
        store.start()
    for store in stores:
        store.wait()


def on_device(
    table, row_state, lookup_grads, lookup_slots, lookup_rows, block_ids, block_counts,
    inputs, cotangent, w_first, w_second,
):
    hbm = pl.BlockSpec(memory_space=pl.ANY)
    shapes = (
        jax.ShapeDtypeStruct((ROWS, EMB), F32),
        jax.ShapeDtypeStruct((BLOCKS, BLOCK_ROWS), F32),
        jax.ShapeDtypeStruct((HID, HID), BF16),
        jax.ShapeDtypeStruct((HID, HID), BF16),
    )
    results = pl.pallas_call(
        kernel,
        out_shape=shapes,
        in_specs=[hbm] * 11,
        out_specs=(hbm,) * 4,
        scratch_shapes=[
            pltpu.VMEM((ROWS, EMB), F32),
            pltpu.VMEM((BLOCKS, BLOCK_ROWS), F32),
            pltpu.VMEM((LOOKUPS, EMB), BF16),
            pltpu.VMEM((1, LOOKUPS), jnp.int32),
            pltpu.VMEM((1, LOOKUPS), jnp.int32),
            pltpu.SMEM((1, SLOTS), jnp.int32),
            pltpu.SMEM((1, 1), jnp.int32),
            pltpu.VMEM((HID, HID), BF16),
            pltpu.VMEM((HID, HID), BF16),
            pltpu.VMEM((2, SAMPLES, HID), BF16),
            pltpu.VMEM((2, SAMPLES, HID), BF16),
            pltpu.VMEM((ROWS, EMB), BF16),
            pltpu.VMEM((Z * C, SHARE, EMB), BF16),
            pltpu.VMEM((ROWS, EMB), F32),
            pltpu.VMEM((4, HID, 128), F32),
            pltpu.VMEM((4, HID, 128), F32),
            pltpu.VMEM((4, HID, 128), F32),
            pltpu.VMEM((X - 1, 2, 128, 128), F32),
            pltpu.VMEM((Y - 1, 64, 128), F32),
            pltpu.VMEM((Z - 1, 64, 128), F32),
            pltpu.VMEM((Y, 24, 128), F32),
            pltpu.VMEM((Z, 24, 128), F32),
            pltpu.VMEM((Y - 1, 24, 128), F32),
            pltpu.VMEM((Z - 1, 24, 128), F32),
            pltpu.VMEM((X, 16, 128), F32),
            pltpu.VMEM((Y, 16, 128), F32),
            pltpu.VMEM((Z, 16, 128), F32),
            pltpu.VMEM((Y, 32, 128), F32),
            pltpu.VMEM((Z, 24, 128), F32),
            pltpu.VMEM((C, X, 264, 128), F32),
            pltpu.VMEM((C, Y, 64, 128), F32),
            pltpu.VMEM((C, Z, 64, 128), F32),
            pltpu.SemaphoreType.DMA((9 + 2 * SAMPLES // CHUNK,)),
            pltpu.SemaphoreType.DMA((4,)),
            pltpu.SemaphoreType.DMA((21,)),
            pltpu.SemaphoreType.DMA((21,)),
        ],
        compiler_params=pltpu.CompilerParams(
            collective_id=0, has_side_effects=True, vmem_limit_bytes=60 * 2**20
        ),
        cost_estimate=pl.CostEstimate(
            flops=2_400_000_000, bytes_accessed=6 * 2**20, transcendentals=2**20
        ),
        name="step",
    )(
        table, row_state.reshape(BLOCKS, BLOCK_ROWS), lookup_grads, lookup_slots, lookup_rows,
        block_ids, block_counts, inputs, cotangent, w_first, w_second,
    )
    new_table, new_state, new_first, new_second = pl.pallas_call(
        hand_over,
        out_shape=shapes,
        in_specs=[hbm] * 4,
        out_specs=(hbm,) * 4,
        scratch_shapes=[pltpu.VMEM(a.shape, a.dtype) for a in shapes]
        + [pltpu.SemaphoreType.DMA((8,))],
        compiler_params=pltpu.CompilerParams(vmem_limit_bytes=60 * 2**20),
        name="hand_over",
    )(*results)
    return (new_table, new_state.reshape(ROWS), new_first, new_second)


def solution(mesh):
    placed = (
        P("table", None),
        P("table"),
        P("replica", "table", None),
        P("replica", "table"),
        P("replica", "table"),
        P("replica", "table"),
        P("replica", "table"),
        P(("replica", "table"), None),
        P(("replica", "table"), None),
        P(),
        P(),
    )
    return jax.shard_map(
        on_device,
        mesh=mesh,
        in_specs=placed,
        out_specs=(P("table", None), P("table"), P(), P()),
        check_vma=False,
    )
```

```python
import jax
import jax.numpy as jnp
from jax import lax
from jax.experimental import pallas as pl
from jax.experimental.pallas import tpu as pltpu
from jax.sharding import PartitionSpec as P

X, Y, Z, C = 4, 8, 8, 2
BLOCK_ROWS = 128
EMB = 128
HID = 512
SLOTS = 4
BLOCKS = 8
SAMPLES = 1024
LOOKUPS = 1024
ROWS = BLOCKS * BLOCK_ROWS
SHARE = ROWS // (Z * C)
CHUNK = 256
PAIR = 22
FAR = {4: (2, 1, 3), 8: (4, 3, 5, 2, 6, 1, 7)}

EMB_RATE = 0.05
MLP_RATE = 0.04 * HID
F32 = jnp.float32
BF16 = jnp.bfloat16
MESH = pl.DeviceIdType.MESH


def kernel(
    table_hbm, state_hbm, grads_hbm, slots_hbm, rows_hbm, ids_hbm, count_hbm,
    inputs_hbm, cot_hbm, w1_hbm, w2_hbm,
    new_table, new_state, new_first, new_second,
    table, state_ref, lgrads, slots_ref, rows_ref, ids_ref, count_ref, w1, w2, left, right,
    dense, emb_recv, merged,
    g_sib, g_own, g_recv,
    r1x, r1y, r1z, t2x, t2y, t2z, r2x, r2y, r2z, r3y, r3z, w4x, w4y, w4z, f5x, f5y, f5z,
    in_sem, send_sem, recv_sem,
):
    rep = lax.axis_index("replica")
    tab = lax.axis_index("table")
    z, c = rep // C, lax.rem(rep, C)
    x, y = tab // Y, lax.rem(tab, Y)
    sib = 1 - c

    def at_x(d):
        return (rep, lax.rem(x + d, X) * Y + y)

    def at_y(d):
        return (rep, x * Y + lax.rem(y + d, Y))

    def at_z(d, core=c):
        return (lax.rem(z + d, Z) * C + core, tab)

    sibling = (z * C + sib, tab)

    opened, taken = {}, set()

    def send(src, dst, k, dev, whole):
        opened[k] = whole
        pltpu.make_async_remote_copy(
            src_ref=src, dst_ref=dst, send_sem=send_sem.at[k], recv_sem=recv_sem.at[k],
            device_id=dev, device_id_type=MESH,
        ).start()

    def take(k):
        taken.add(k)
        pltpu.make_async_copy(opened[k], opened[k], recv_sem.at[k]).wait()

    def finish():
        for k, whole in opened.items():
            if k not in taken:
                take(k)
            pltpu.make_async_copy(whole, whole, send_sem.at[k]).wait()

    parts = [pl.ds(k * CHUNK, CHUNK) for k in range(SAMPLES // CHUNK)]
    pairs = [
        (count_hbm, count_ref), (ids_hbm, ids_ref), (slots_hbm, slots_ref), (rows_hbm, rows_ref),
        (grads_hbm.at[0], lgrads), (w1_hbm, w1), (w2_hbm, w2),
    ]
    for rows in parts:
        pairs += [(inputs_hbm.at[rows], left.at[0, rows]), (cot_hbm.at[rows], right.at[1, rows])]
    pairs += [(state_hbm, state_ref), (table_hbm, table)]
    loads = [pltpu.make_async_copy(*pair, in_sem.at[k]) for k, pair in enumerate(pairs)]
    for load in loads:
        load.start()

    barrier = pltpu.get_barrier_semaphore()
    peers = [at_x(d) for d in range(1, X)] + [at_y(d) for d in range(1, Y)]
    peers += [at_z(d) for d in range(1, Z)] + [at_z(d, sib) for d in range(Z)]
    for dev in peers:
        pl.semaphore_signal(barrier, inc=1, device_id=dev, device_id_type=MESH)

    for load in loads[:5]:
        load.wait()
    count = count_ref[0, 0]
    slot_ids = slots_ref[...]
    position = jnp.where(slot_ids < count, slot_ids * BLOCK_ROWS + rows_ref[...], -1)
    lookup_grads = lgrads[...]
    slot_sums = []
    for k in range(SLOTS):
        target = lax.broadcasted_iota(jnp.int32, (BLOCK_ROWS, LOOKUPS), 0) + k * BLOCK_ROWS
        onehot = jnp.where(target == position, 1.0, 0.0).astype(BF16)
        found = jnp.dot(onehot, lookup_grads, preferred_element_type=F32)
        slot_sums.append(found.astype(BF16).astype(F32))
    for b in range(BLOCKS):
        block = jnp.zeros((BLOCK_ROWS, EMB), F32)
        for k in range(SLOTS):
            block += jnp.where((ids_ref[0, k] == b) & (k < count), 1.0, 0.0) * slot_sums[k]
        dense[pl.ds(b * BLOCK_ROWS, BLOCK_ROWS)] = block.astype(BF16)

    def share(zz, cc):
        return pl.ds(pl.multiple_of((cc * Z + zz) * SHARE, SHARE), SHARE)

    pl.semaphore_wait(barrier, len(peers))
    for d in FAR[Z] + (0,):
        for core in (c, sib):
            if d == 0 and core is c:
                continue
            send(
                dense.at[share(lax.rem(z + d, Z), core)], emb_recv.at[rep], 0, at_z(d, core),
                emb_recv.at[pl.ds(0, Z * C - 1)],
            )
    emb_recv[rep] = dense[share(z, c)]

    loads[5].wait()
    loads[6].wait()
    for k, rows in enumerate(parts):
        loads[7 + 2 * k].wait()
        loads[8 + 2 * k].wait()
        pre = jnp.dot(left[0, rows], w1[...], preferred_element_type=F32)
        back = lax.dot_general(
            right[1, rows], w2[...], (((1,), (1,)), ((), ())), preferred_element_type=F32
        )
        sig = jax.nn.sigmoid(pre)
        left[1, rows] = (pre * sig).astype(BF16)
        right[0, rows] = (back * sig * (1.0 + pre * (1.0 - sig))).astype(BF16)

    def grad(which, half):
        cols = pl.ds(half * 256, 256)
        return lax.dot_general(
            left[which], right[which, :, cols], (((0,), (0,)), ((), ())),
            preferred_element_type=F32,
        )

    for half in (1, 0):
        g = grad(sib, half)
        for k in range(2):
            block = 2 * half + k
            g_sib[block] = g[:, 128 * k:128 * k + 128]
            send(g_sib.at[block], g_recv.at[block], PAIR + block, sibling, g_recv.at[block])
    for half in (1, 0):
        g = grad(c, half)
        g_own[2 * half] = g[:, :128]
        g_own[2 * half + 1] = g[:, 128:]

    def piece(k, rows):
        return pl.ds(pl.multiple_of(k * rows, rows), rows)

    take(PAIR + 2)
    g_own[2] = g_own[2] + g_recv[2]
    for d in FAR[Y]:
        send(g_own.at[2, piece(lax.rem(y + d, Y), 64)], r1y.at[d - 1], 5, at_y(d), r1y)
    take(PAIR + 3)
    g_own[3] = g_own[3] + g_recv[3]
    for d in FAR[Z]:
        send(g_own.at[3, piece(lax.rem(z + d, Z), 64)], r1z.at[d - 1], 6, at_z(d), r1z)
    take(PAIR)
    take(PAIR + 1)
    g_own[0:2] = g_own[0:2] + g_recv[0:2]
    for d in FAR[X]:
        rows = piece(lax.rem(x + d, X), 128)
        send(g_own.at[pl.ds(0, 2), rows], r1x.at[d - 1], 4, at_x(d), r1x)

    def summed(ref, n, first):
        for k in range(n):
            first = first + ref[k]
        return first

    take(0)
    total = emb_recv[0].astype(F32)
    for k in range(1, Z * C):
        total += emb_recv[k].astype(F32)
    merged[share(z, c)] = total
    r3z[z, 32:40] = jnp.sum((total * total).reshape(SHARE // 8, 8, EMB), axis=0)

    take(4)
    s = summed(r1x, X - 1, g_own[0:2, piece(x, 128)])
    t2y[...] = s[0].reshape(Y, 16, 128)
    t2z[...] = s[1].reshape(Z, 16, 128)
    for d in FAR[Y]:
        send(t2y.at[lax.rem(y + d, Y)], r2y.at[d - 1], 9, at_y(d), r2y)
        send(t2z.at[lax.rem(z + d, Z)], r2z.at[d - 1], 8, at_z(d), r2z)
    for d in (2, 6, 1, 7):
        send(
            merged.at[share(z, c)], merged.at[share(z, c)], 3, at_z(d),
            merged.at[pl.ds(0, SHARE * (Z - 1))],
        )

    take(5)
    t2x[:, 0:16] = summed(r1y, Y - 1, g_own[2, piece(y, 64)]).reshape(X, 16, 128)
    take(6)
    t2x[:, 16:32] = summed(r1z, Z - 1, g_own[3, piece(z, 64)]).reshape(X, 16, 128)
    for d in FAR[X]:
        send(t2x.at[lax.rem(x + d, X)], r2x.at[d - 1], 7, at_x(d), r2x)

    take(9)
    r3z[z, 0:16] = summed(r2y, Y - 1, t2y[y])
    take(8)
    r3y[y, 0:16] = summed(r2z, Z - 1, t2z[z])
    take(7)
    s = summed(r2x, X - 1, t2x[x])
    r3z[z, 16:32] = s[0:16]
    r3y[y, 16:32] = s[16:32]
    for d in FAR[Y]:
        send(r3z.at[z], r3z.at[z], 11, at_z(d), r3z.at[pl.ds(0, Z - 1)])
        send(r3y.at[y], r3y.at[y], 10, at_y(d), r3y.at[pl.ds(0, Y - 1)])

    take(11)
    s = summed(r3z, Z, 0.0)
    w4y[y, 0:16] = s[0:16]
    w4y[y, 16:24] = s[32:40]
    w4x[x, 0:16] = s[16:32]
    for d in FAR[Y]:
        send(w4y.at[y], w4y.at[y], 14, at_y(d), w4y.at[pl.ds(0, Y - 1)])
    take(10)
    s = summed(r3y, Y, 0.0)
    w4z[z] = s[0:16]
    w4x[x, 16:32] = s[16:32]
    for d in FAR[X]:
        send(w4x.at[x], w4x.at[x], 12, at_x(d), w4x.at[pl.ds(0, X - 1)])
    for d in FAR[Z]:
        send(w4z.at[z], w4z.at[z], 13, at_z(d), w4z.at[pl.ds(0, Z - 1)])

    for d in (4, 3, 5):
        send(
            merged.at[share(z, c)], merged.at[share(z, c)], 3, at_z(d),
            merged.at[pl.ds(0, SHARE * (Z - 1))],
        )

    take(12)
    f5y[c, y] = w4x[:, 0:16].reshape(64, 128)
    f5z[c, z] = w4x[:, 16:32].reshape(64, 128)
    for d in FAR[Y]:
        send(f5y.at[c, y], f5y.at[c, y], 15, at_y(d), f5y.at[0, pl.ds(0, Y - 1)])
        send(f5z.at[c, z], f5z.at[c, z], 17, at_z(d), f5z.at[0, pl.ds(0, Z - 1)])

    half_rows = piece(c, ROWS // 2)
    take(3)
    send(merged.at[half_rows], merged.at[half_rows], 18, sibling, merged.at[half_rows])
    lane = lax.broadcasted_iota(jnp.int32, (BLOCK_ROWS, 128), 1)

    def squares_of(core):
        found = jnp.zeros((BLOCK_ROWS, 128), F32)
        for k in range(BLOCKS // C):
            b = core * (BLOCKS // C) + k
            m = merged[piece(b, BLOCK_ROWS)]
            found = jnp.where(lane == b, jnp.sum(m * m, axis=1, keepdims=True), found)
        return found

    take(14)
    f5x[c, x, 0:128] = w4y[:, 0:16].reshape(128, 128)
    f5x[c, x, 256:264] = jnp.sum(w4y[:, 16:24], axis=0)
    take(13)
    f5x[c, x, 128:256] = w4z[...].reshape(128, 128)
    for d in FAR[X]:
        send(f5x.at[c, x], f5x.at[c, x], 16, at_x(d), f5x.at[0, pl.ds(0, X - 1)])

    squares = squares_of(c)
    take(18)
    squares = (squares + squares_of(sib)) * (1.0 / EMB)
    squares_row = jnp.transpose(squares)[0:BLOCKS]
    loads[-2].wait()
    state_row = state_ref[...]
    state_col = jnp.transpose(
        jnp.concatenate([state_row, jnp.zeros((BLOCK_ROWS - BLOCKS, 128), F32)], axis=0)
    )

    def squared(core, ref, n, rows):
        found = jnp.zeros((64, 128), F32)
        for k in range(n):
            for q in range(rows // 64):
                v = ref[core, k, 64 * q:64 * q + 64]
                found += v * v
        return found

    take(16)
    send(f5x.at[c], f5x.at[c], 19, sibling, f5x.at[0])
    take(15)
    send(f5y.at[c], f5y.at[c], 20, sibling, f5y.at[0])
    take(17)
    send(f5z.at[c], f5z.at[c], 21, sibling, f5z.at[0])
    mine = squared(c, f5y, Y, 64) + squared(c, f5z, Z, 64) + squared(c, f5x, X, 256)
    loads[-1].wait()
    take(19)
    take(20)
    take(21)
    other = squared(sib, f5y, Y, 64) + squared(sib, f5z, Z, 64) + squared(sib, f5x, X, 256)

    emb = f5x[:, :, 256:264]
    total = jnp.sum(mine + other, keepdims=True)
    total = total + jnp.sum(jnp.sum(emb, axis=(0, 1)), keepdims=True)
    clip = jnp.minimum(1.0, 1.0 / (jnp.sqrt(total) + 1e-06))

    clip_sq = clip * clip
    scale = (EMB_RATE * clip) / jnp.sqrt(state_col + clip_sq * squares)
    for b in range(BLOCKS):
        rows = pl.ds(b * BLOCK_ROWS, BLOCK_ROWS)
        new_table[rows] = table[rows] - merged[rows] * scale[:, b:b + 1]
    new_state[...] = state_row + clip_sq * squares_row
    rate = MLP_RATE * clip
    for core, (w, out) in enumerate(((w1, new_first), (w2, new_second))):
        for q in range(2):
            cols = pl.ds(128 * q, 128)
            for k in range(X):
                rows = pl.ds(128 * k, 128)
                g = f5x[core, k, 128 * q:128 * q + 128]
                out[rows, cols] = (w[rows, cols].astype(F32) - rate * g).astype(BF16)
        for q, ref in ((2, f5y), (3, f5z)):
            cols = pl.ds(128 * q, 128)
            g = ref[core].reshape(HID, 128)
            out[:, cols] = (w[:, cols].astype(F32) - rate * g).astype(BF16)
    finish()


def hand_over(*refs):
    *arrays, sem = refs
    n = len(arrays) // 2
    copies = [pltpu.make_async_copy(arrays[k], arrays[n + k], sem.at[k]) for k in range(n)]
    for copy in copies:
        copy.start()
    for copy in copies:
        copy.wait()


def on_device(
    table, row_state, lookup_grads, lookup_slots, lookup_rows, block_ids, block_counts,
    inputs, cotangent, w_first, w_second,
):
    hbm = pl.BlockSpec(memory_space=pl.ANY)
    vmem = pl.BlockSpec(memory_space=pltpu.VMEM)
    shapes = (
        jax.ShapeDtypeStruct((ROWS, EMB), F32),
        jax.ShapeDtypeStruct((BLOCKS, BLOCK_ROWS), F32),
        jax.ShapeDtypeStruct((HID, HID), BF16),
        jax.ShapeDtypeStruct((HID, HID), BF16),
    )
    results = pl.pallas_call(
        kernel,
        out_shape=tuple(pltpu.VMEM(a.shape, a.dtype) for a in shapes),
        in_specs=[hbm] * 11,
        out_specs=(vmem,) * 4,
        scratch_shapes=[
            pltpu.VMEM((ROWS, EMB), F32),
            pltpu.VMEM((BLOCKS, BLOCK_ROWS), F32),
            pltpu.VMEM((LOOKUPS, EMB), BF16),
            pltpu.VMEM((1, LOOKUPS), jnp.int32),
            pltpu.VMEM((1, LOOKUPS), jnp.int32),
            pltpu.SMEM((1, SLOTS), jnp.int32),
            pltpu.SMEM((1, 1), jnp.int32),
            pltpu.VMEM((HID, HID), BF16),
            pltpu.VMEM((HID, HID), BF16),
            pltpu.VMEM((2, SAMPLES, HID), BF16),
            pltpu.VMEM((2, SAMPLES, HID), BF16),
            pltpu.VMEM((ROWS, EMB), BF16),
            pltpu.VMEM((Z * C, SHARE, EMB), BF16),
            pltpu.VMEM((ROWS, EMB), F32),
            pltpu.VMEM((4, HID, 128), F32),
            pltpu.VMEM((4, HID, 128), F32),
            pltpu.VMEM((4, HID, 128), F32),
            pltpu.VMEM((X - 1, 2, 128, 128), F32),
            pltpu.VMEM((Y - 1, 64, 128), F32),
            pltpu.VMEM((Z - 1, 64, 128), F32),
            pltpu.VMEM((X, 32, 128), F32),
            pltpu.VMEM((Y, 16, 128), F32),
            pltpu.VMEM((Z, 16, 128), F32),
            pltpu.VMEM((X - 1, 32, 128), F32),
            pltpu.VMEM((Y - 1, 16, 128), F32),
            pltpu.VMEM((Z - 1, 16, 128), F32),
            pltpu.VMEM((Y, 32, 128), F32),
            pltpu.VMEM((Z, 40, 128), F32),
            pltpu.VMEM((X, 32, 128), F32),
            pltpu.VMEM((Y, 24, 128), F32),
            pltpu.VMEM((Z, 16, 128), F32),
            pltpu.VMEM((C, X, 264, 128), F32),
            pltpu.VMEM((C, Y, 64, 128), F32),
            pltpu.VMEM((C, Z, 64, 128), F32),
            pltpu.SemaphoreType.DMA((9 + 2 * SAMPLES // CHUNK,)),
            pltpu.SemaphoreType.DMA((26,)),
            pltpu.SemaphoreType.DMA((26,)),
        ],
        compiler_params=pltpu.CompilerParams(
            collective_id=0, has_side_effects=True, vmem_limit_bytes=60 * 2**20
        ),
        cost_estimate=pl.CostEstimate(
            flops=2_400_000_000, bytes_accessed=6 * 2**20, transcendentals=2**20
        ),
        name="step",
    )(
        table, row_state.reshape(BLOCKS, BLOCK_ROWS), lookup_grads, lookup_slots, lookup_rows,
        block_ids, block_counts, inputs, cotangent, w_first, w_second,
    )
    new_table, new_state, new_first, new_second = pl.pallas_call(
        hand_over,
        out_shape=shapes,
        in_specs=[vmem] * 4,
        out_specs=(hbm,) * 4,
        scratch_shapes=[pltpu.SemaphoreType.DMA((4,))],
        compiler_params=pltpu.CompilerParams(vmem_limit_bytes=16 * 2**20),
        name="hand_over",
    )(*results)
    return (new_table, new_state.reshape(ROWS), new_first, new_second)


def solution(mesh):
    placed = (
        P("table", None),
        P("table"),
        P("replica", "table", None),
        P("replica", "table"),
        P("replica", "table"),
        P("replica", "table"),
        P("replica", "table"),
        P(("replica", "table"), None),
        P(("replica", "table"), None),
        P(),
        P(),
    )
    return jax.shard_map(
        on_device,
        mesh=mesh,
        in_specs=placed,
        out_specs=(P("table", None), P("table"), P(), P()),
        check_vma=False,
    )
```

```python
import jax
import jax.numpy as jnp
from jax import lax
from jax.experimental import pallas as pl
from jax.experimental.pallas import tpu as pltpu
from jax.sharding import PartitionSpec as P

X, Y, Z, C = 4, 8, 8, 2
BLOCK_ROWS = 128
EMB = 128
HID = 512
SLOTS = 4
BLOCKS = 8
SAMPLES = 1024
LOOKUPS = 1024
ROWS = BLOCKS * BLOCK_ROWS
SHARE = ROWS // (Z * C)
CHUNK = 256
PAIR = 23
FAR = {4: (2, 1, 3), 8: (4, 3, 5, 2, 6, 1, 7)}

EMB_RATE = 0.05
MLP_RATE = 0.04 * HID
F32 = jnp.float32
BF16 = jnp.bfloat16
MESH = pl.DeviceIdType.MESH


def kernel(
    table_hbm, state_hbm, grads_hbm, slots_hbm, rows_hbm, ids_hbm, count_hbm,
    inputs_hbm, cot_hbm, w1_hbm, w2_hbm,
    new_table, new_state, new_first, new_second,
    table, state_ref, lgrads, slots_ref, rows_ref, ids_ref, count_ref, w1, w2, left, right,
    dense, emb_recv, merged,
    g_sib, g_own, g_recv,
    r1x, r1y, r1z, t2x, t2y, t2z, r2x, r2y, r2z, r3y, r3z, w4x, w4y, w4z, f5x, f5y, f5z,
    in_sem, send_sem, recv_sem,
):
    rep = lax.axis_index("replica")
    tab = lax.axis_index("table")
    z, c = rep // C, lax.rem(rep, C)
    x, y = tab // Y, lax.rem(tab, Y)
    sib = 1 - c

    def at_x(d):
        return (rep, lax.rem(x + d, X) * Y + y)

    def at_y(d):
        return (rep, x * Y + lax.rem(y + d, Y))

    def at_z(d, core=c):
        return (lax.rem(z + d, Z) * C + core, tab)

    sibling = (z * C + sib, tab)

    opened, taken = {}, set()

    def send(src, dst, k, dev, whole):
        opened[k] = whole
        pltpu.make_async_remote_copy(
            src_ref=src, dst_ref=dst, send_sem=send_sem.at[k], recv_sem=recv_sem.at[k],
            device_id=dev, device_id_type=MESH,
        ).start()

    def take(k):
        taken.add(k)
        pltpu.make_async_copy(opened[k], opened[k], recv_sem.at[k]).wait()

    def finish():
        for k, whole in opened.items():
            if k not in taken:
                take(k)
            pltpu.make_async_copy(whole, whole, send_sem.at[k]).wait()

    barrier = pltpu.get_barrier_semaphore()
    peers = [at_x(d) for d in range(1, X)] + [at_y(d) for d in range(1, Y)]
    peers += [at_z(d) for d in range(1, Z)] + [at_z(d, sib) for d in range(Z)]
    for dev in peers:
        pl.semaphore_signal(barrier, inc=1, device_id=dev, device_id_type=MESH)

    parts = [pl.ds(k * CHUNK, CHUNK) for k in range(SAMPLES // CHUNK)]
    pairs = [
        (count_hbm, count_ref), (ids_hbm, ids_ref), (slots_hbm, slots_ref), (rows_hbm, rows_ref),
        (grads_hbm.at[0], lgrads), (w1_hbm, w1), (w2_hbm, w2),
    ]
    for rows in parts:
        pairs += [(inputs_hbm.at[rows], left.at[0, rows]), (cot_hbm.at[rows], right.at[1, rows])]
    pairs += [(state_hbm, state_ref), (table_hbm, table)]
    loads = [pltpu.make_async_copy(*pair, in_sem.at[k]) for k, pair in enumerate(pairs)]
    for load in loads:
        load.start()

    for load in loads[:5]:
        load.wait()
    count = count_ref[0, 0]
    slot_ids = slots_ref[...]
    position = jnp.where(slot_ids < count, slot_ids * BLOCK_ROWS + rows_ref[...], -1)
    lookup_grads = lgrads[...]
    slot_sums = []
    for k in range(SLOTS):
        target = lax.broadcasted_iota(jnp.int32, (BLOCK_ROWS, LOOKUPS), 0) + k * BLOCK_ROWS
        onehot = jnp.where(target == position, 1.0, 0.0).astype(BF16)
        found = jnp.dot(onehot, lookup_grads, preferred_element_type=F32)
        slot_sums.append(found.astype(BF16).astype(F32))
    for b in range(BLOCKS):
        block = jnp.zeros((BLOCK_ROWS, EMB), F32)
        for k in range(SLOTS):
            block += jnp.where((ids_ref[0, k] == b) & (k < count), 1.0, 0.0) * slot_sums[k]
        dense[pl.ds(b * BLOCK_ROWS, BLOCK_ROWS)] = block.astype(BF16)

    def share(zz, cc):
        return pl.ds(pl.multiple_of((cc * Z + zz) * SHARE, SHARE), SHARE)

    pl.semaphore_wait(barrier, len(peers))
    for d in FAR[Z] + (0,):
        for core in (c, sib):
            if d == 0 and core is c:
                continue
            send(
                dense.at[share(lax.rem(z + d, Z), core)], emb_recv.at[rep], 0, at_z(d, core),
                emb_recv.at[pl.ds(0, Z * C - 1)],
            )
    emb_recv[rep] = dense[share(z, c)]

    loads[5].wait()
    loads[6].wait()
    for k, rows in enumerate(parts):
        loads[7 + 2 * k].wait()
        loads[8 + 2 * k].wait()
        pre = jnp.dot(left[0, rows], w1[...], preferred_element_type=F32)
        back = lax.dot_general(
            right[1, rows], w2[...], (((1,), (1,)), ((), ())), preferred_element_type=F32
        )
        sig = jax.nn.sigmoid(pre)
        left[1, rows] = (pre * sig).astype(BF16)
        right[0, rows] = (back * sig * (1.0 + pre * (1.0 - sig))).astype(BF16)

    def grad(which, half):
        cols = pl.ds(half * 256, 256)
        return lax.dot_general(
            left[which], right[which, :, cols], (((0,), (0,)), ((), ())),
            preferred_element_type=F32,
        )

    for half in (1, 0):
        g = grad(sib, half)
        for k in range(2):
            block = 2 * half + k
            g_sib[block] = g[:, 128 * k:128 * k + 128]
            send(g_sib.at[block], g_recv.at[block], PAIR + block, sibling, g_recv.at[block])
    for half in (1, 0):
        g = grad(c, half)
        g_own[2 * half] = g[:, :128]
        g_own[2 * half + 1] = g[:, 128:]

    def piece(k, rows):
        return pl.ds(pl.multiple_of(k * rows, rows), rows)

    take(PAIR + 2)
    g_own[2] = g_own[2] + g_recv[2]
    for d in FAR[Y]:
        send(g_own.at[2, piece(lax.rem(y + d, Y), 64)], r1y.at[d - 1], 5, at_y(d), r1y)
    take(PAIR + 3)
    g_own[3] = g_own[3] + g_recv[3]
    for d in FAR[Z]:
        send(g_own.at[3, piece(lax.rem(z + d, Z), 64)], r1z.at[d - 1], 6, at_z(d), r1z)
    take(PAIR)
    take(PAIR + 1)
    g_own[0:2] = g_own[0:2] + g_recv[0:2]
    for d in FAR[X]:
        rows = piece(lax.rem(x + d, X), 128)
        send(g_own.at[pl.ds(0, 2), rows], r1x.at[d - 1], 4, at_x(d), r1x)

    def summed(ref, n, first):
        for k in range(n):
            first = first + ref[k]
        return first

    take(0)
    total = emb_recv[0].astype(F32)
    for k in range(1, Z * C):
        total += emb_recv[k].astype(F32)
    merged[share(z, c)] = total
    r3z[z, 32:40] = jnp.sum((total * total).reshape(SHARE // 8, 8, EMB), axis=0)

    take(4)
    s = summed(r1x, X - 1, g_own[0:2, piece(x, 128)])
    t2y[...] = s[0].reshape(Y, 16, 128)
    t2z[...] = s[1].reshape(Z, 16, 128)
    for d in FAR[Y]:
        send(t2y.at[lax.rem(y + d, Y)], r2y.at[d - 1], 9, at_y(d), r2y)
        send(t2z.at[lax.rem(z + d, Z)], r2z.at[d - 1], 8, at_z(d), r2z)
    for d in (2, 6, 1, 7):
        send(
            merged.at[share(z, c)], merged.at[share(z, c)], 3, at_z(d), merged.at[pl.ds(0, 4 * SHARE)]
        )

    take(5)
    t2x[:, 0:16] = summed(r1y, Y - 1, g_own[2, piece(y, 64)]).reshape(X, 16, 128)
    take(6)
    t2x[:, 16:32] = summed(r1z, Z - 1, g_own[3, piece(z, 64)]).reshape(X, 16, 128)
    for d in FAR[X]:
        send(t2x.at[lax.rem(x + d, X)], r2x.at[d - 1], 7, at_x(d), r2x)

    take(9)
    r3z[z, 0:16] = summed(r2y, Y - 1, t2y[y])
    take(8)
    r3y[y, 0:16] = summed(r2z, Z - 1, t2z[z])
    take(7)
    s = summed(r2x, X - 1, t2x[x])
    r3z[z, 16:32] = s[0:16]
    r3y[y, 16:32] = s[16:32]
    for d in FAR[Y]:
        send(r3z.at[z], r3z.at[z], 11, at_z(d), r3z.at[pl.ds(0, Z - 1)])
        send(r3y.at[y], r3y.at[y], 10, at_y(d), r3y.at[pl.ds(0, Y - 1)])

    take(11)
    s = summed(r3z, Z, 0.0)
    w4y[y, 0:16] = s[0:16]
    w4y[y, 16:24] = s[32:40]
    w4x[x, 0:16] = s[16:32]
    for d in FAR[Y]:
        send(w4y.at[y], w4y.at[y], 14, at_y(d), w4y.at[pl.ds(0, Y - 1)])
    take(10)
    s = summed(r3y, Y, 0.0)
    w4z[z] = s[0:16]
    w4x[x, 16:32] = s[16:32]
    for d in FAR[X]:
        send(w4x.at[x], w4x.at[x], 12, at_x(d), w4x.at[pl.ds(0, X - 1)])
    for d in FAR[Z]:
        send(w4z.at[z], w4z.at[z], 13, at_z(d), w4z.at[pl.ds(0, Z - 1)])

    take(3)
    up, down = share(lax.rem(z + 2, Z), c), share(lax.rem(z + 6, Z), c)
    start = (c * Z) * SHARE
    up_half = pl.ds(pl.multiple_of(start + lax.rem(z + 2, Z) * SHARE, 32), SHARE // 2)
    down_half = pl.ds(
        pl.multiple_of(start + lax.rem(z + 6, Z) * SHARE + SHARE // 2, 32), SHARE // 2
    )
    for rows, d in ((up_half, 6), (down_half, 2), (up, 7), (down, 1)):
        send(merged.at[rows], merged.at[rows], 22, at_z(d), merged.at[pl.ds(0, 3 * SHARE)])

    take(12)
    f5y[c, y] = w4x[:, 0:16].reshape(64, 128)
    f5z[c, z] = w4x[:, 16:32].reshape(64, 128)
    for d in FAR[Y]:
        send(f5y.at[c, y], f5y.at[c, y], 15, at_y(d), f5y.at[0, pl.ds(0, Y - 1)])
        send(f5z.at[c, z], f5z.at[c, z], 17, at_z(d), f5z.at[0, pl.ds(0, Z - 1)])

    half_rows = piece(c, ROWS // 2)
    take(22)
    send(merged.at[half_rows], merged.at[half_rows], 18, sibling, merged.at[half_rows])
    lane = lax.broadcasted_iota(jnp.int32, (BLOCK_ROWS, 128), 1)

    def squares_of(core):
        found = jnp.zeros((BLOCK_ROWS, 128), F32)
        for k in range(BLOCKS // C):
            b = core * (BLOCKS // C) + k
            m = merged[piece(b, BLOCK_ROWS)]
            found = jnp.where(lane == b, jnp.sum(m * m, axis=1, keepdims=True), found)
        return found

    take(14)
    f5x[c, x, 0:128] = w4y[:, 0:16].reshape(128, 128)
    f5x[c, x, 256:264] = jnp.sum(w4y[:, 16:24], axis=0)
    take(13)
    f5x[c, x, 128:256] = w4z[...].reshape(128, 128)
    for d in FAR[X]:
        send(f5x.at[c, x], f5x.at[c, x], 16, at_x(d), f5x.at[0, pl.ds(0, X - 1)])

    squares = squares_of(c)
    take(18)
    squares = (squares + squares_of(sib)) * (1.0 / EMB)
    squares_row = jnp.transpose(squares)[0:BLOCKS]
    loads[-2].wait()
    state_row = state_ref[...]
    state_col = jnp.transpose(
        jnp.concatenate([state_row, jnp.zeros((BLOCK_ROWS - BLOCKS, 128), F32)], axis=0)
    )

    def squared(core, ref, n, rows):
        found = jnp.zeros((64, 128), F32)
        for k in range(n):
            for q in range(rows // 64):
                v = ref[core, k, 64 * q:64 * q + 64]
                found += v * v
        return found

    take(16)
    send(f5x.at[c], f5x.at[c], 19, sibling, f5x.at[0])
    take(15)
    send(f5y.at[c], f5y.at[c], 20, sibling, f5y.at[0])
    take(17)
    send(f5z.at[c], f5z.at[c], 21, sibling, f5z.at[0])
    mine = squared(c, f5y, Y, 64) + squared(c, f5z, Z, 64) + squared(c, f5x, X, 256)
    loads[-1].wait()
    take(19)
    take(20)
    take(21)
    other = squared(sib, f5y, Y, 64) + squared(sib, f5z, Z, 64) + squared(sib, f5x, X, 256)

    emb = f5x[:, :, 256:264]
    total = jnp.sum(mine + other, keepdims=True)
    total = total + jnp.sum(jnp.sum(emb, axis=(0, 1)), keepdims=True)
    clip = jnp.minimum(1.0, 1.0 / (jnp.sqrt(total) + 1e-06))

    clip_sq = clip * clip
    scale = (EMB_RATE * clip) / jnp.sqrt(state_col + clip_sq * squares)
    for b in range(BLOCKS):
        rows = pl.ds(b * BLOCK_ROWS, BLOCK_ROWS)
        new_table[rows] = table[rows] - merged[rows] * scale[:, b:b + 1]
    new_state[...] = state_row + clip_sq * squares_row
    rate = MLP_RATE * clip
    for core, (w, out) in enumerate(((w1, new_first), (w2, new_second))):
        for q in range(2):
            cols = pl.ds(128 * q, 128)
            for k in range(X):
                rows = pl.ds(128 * k, 128)
                g = f5x[core, k, 128 * q:128 * q + 128]
                out[rows, cols] = (w[rows, cols].astype(F32) - rate * g).astype(BF16)
        for q, ref in ((2, f5y), (3, f5z)):
            cols = pl.ds(128 * q, 128)
            g = ref[core].reshape(HID, 128)
            out[:, cols] = (w[:, cols].astype(F32) - rate * g).astype(BF16)
    finish()


def hand_over(*refs):
    *arrays, sem = refs
    n = len(arrays) // 2
    copies = [pltpu.make_async_copy(arrays[k], arrays[n + k], sem.at[k]) for k in range(n)]
    for copy in copies:
        copy.start()
    for copy in copies:
        copy.wait()


def on_device(
    table, row_state, lookup_grads, lookup_slots, lookup_rows, block_ids, block_counts,
    inputs, cotangent, w_first, w_second,
):
    hbm = pl.BlockSpec(memory_space=pl.ANY)
    vmem = pl.BlockSpec(memory_space=pltpu.VMEM)
    shapes = (
        jax.ShapeDtypeStruct((ROWS, EMB), F32),
        jax.ShapeDtypeStruct((BLOCKS, BLOCK_ROWS), F32),
        jax.ShapeDtypeStruct((HID, HID), BF16),
        jax.ShapeDtypeStruct((HID, HID), BF16),
    )
    results = pl.pallas_call(
        kernel,
        out_shape=tuple(pltpu.VMEM(a.shape, a.dtype) for a in shapes),
        in_specs=[hbm] * 11,
        out_specs=(vmem,) * 4,
        scratch_shapes=[
            pltpu.VMEM((ROWS, EMB), F32),
            pltpu.VMEM((BLOCKS, BLOCK_ROWS), F32),
            pltpu.VMEM((LOOKUPS, EMB), BF16),
            pltpu.VMEM((1, LOOKUPS), jnp.int32),
            pltpu.VMEM((1, LOOKUPS), jnp.int32),
            pltpu.SMEM((1, SLOTS), jnp.int32),
            pltpu.SMEM((1, 1), jnp.int32),
            pltpu.VMEM((HID, HID), BF16),
            pltpu.VMEM((HID, HID), BF16),
            pltpu.VMEM((2, SAMPLES, HID), BF16),
            pltpu.VMEM((2, SAMPLES, HID), BF16),
            pltpu.VMEM((ROWS, EMB), BF16),
            pltpu.VMEM((Z * C, SHARE, EMB), BF16),
            pltpu.VMEM((ROWS, EMB), F32),
            pltpu.VMEM((4, HID, 128), F32),
            pltpu.VMEM((4, HID, 128), F32),
            pltpu.VMEM((4, HID, 128), F32),
            pltpu.VMEM((X - 1, 2, 128, 128), F32),
            pltpu.VMEM((Y - 1, 64, 128), F32),
            pltpu.VMEM((Z - 1, 64, 128), F32),
            pltpu.VMEM((X, 32, 128), F32),
            pltpu.VMEM((Y, 16, 128), F32),
            pltpu.VMEM((Z, 16, 128), F32),
            pltpu.VMEM((X - 1, 32, 128), F32),
            pltpu.VMEM((Y - 1, 16, 128), F32),
            pltpu.VMEM((Z - 1, 16, 128), F32),
            pltpu.VMEM((Y, 32, 128), F32),
            pltpu.VMEM((Z, 40, 128), F32),
            pltpu.VMEM((X, 32, 128), F32),
            pltpu.VMEM((Y, 24, 128), F32),
            pltpu.VMEM((Z, 16, 128), F32),
            pltpu.VMEM((C, X, 264, 128), F32),
            pltpu.VMEM((C, Y, 64, 128), F32),
            pltpu.VMEM((C, Z, 64, 128), F32),
            pltpu.SemaphoreType.DMA((9 + 2 * SAMPLES // CHUNK,)),
            pltpu.SemaphoreType.DMA((27,)),
            pltpu.SemaphoreType.DMA((27,)),
        ],
        compiler_params=pltpu.CompilerParams(
            collective_id=0, has_side_effects=True, vmem_limit_bytes=60 * 2**20
        ),
        cost_estimate=pl.CostEstimate(
            flops=2_400_000_000, bytes_accessed=6 * 2**20, transcendentals=2**20
        ),
        name="step",
    )(
        table, row_state.reshape(BLOCKS, BLOCK_ROWS), lookup_grads, lookup_slots, lookup_rows,
        block_ids, block_counts, inputs, cotangent, w_first, w_second,
    )
    new_table, new_state, new_first, new_second = pl.pallas_call(
        hand_over,
        out_shape=shapes,
        in_specs=[vmem] * 4,
        out_specs=(hbm,) * 4,
        scratch_shapes=[pltpu.SemaphoreType.DMA((4,))],
        compiler_params=pltpu.CompilerParams(vmem_limit_bytes=16 * 2**20),
        name="hand_over",
    )(*results)
    return (new_table, new_state.reshape(ROWS), new_first, new_second)


def solution(mesh):
    placed = (
        P("table", None),
        P("table"),
        P("replica", "table", None),
        P("replica", "table"),
        P("replica", "table"),
        P("replica", "table"),
        P("replica", "table"),
        P(("replica", "table"), None),
        P(("replica", "table"), None),
        P(),
        P(),
    )
    return jax.shard_map(
        on_device,
        mesh=mesh,
        in_specs=placed,
        out_specs=(P("table", None), P("table"), P(), P()),
        check_vma=False,
    )
```

```python
import jax
import jax.numpy as jnp
from jax import lax
from jax.experimental import pallas as pl
from jax.experimental.pallas import tpu as pltpu
from jax.sharding import PartitionSpec as P

X, Y, Z, C = 4, 8, 8, 2
BLOCK_ROWS = 128
EMB = 128
HID = 512
SLOTS = 4
BLOCKS = 8
SAMPLES = 1024
LOOKUPS = 1024
ROWS = BLOCKS * BLOCK_ROWS
SHARE = ROWS // (Z * C)
CHUNK = 256
PAIR = 23
XA, XD, YB, ZB = 512, 512, 768, 256
AT_D = XA
AT_B = XA + XD
AT_Z = XA + XD + YB
PA, PD, PB, PZ = XA // X, XD // X, YB // Y, ZB // Z
QA, QD, QB, QZ = PA // Y, PD // Z, PB // X, PZ // X
PX = PA + PD
FAR = {4: (2, 1, 3), 8: (4, 3, 5, 2, 6, 1, 7)}

EMB_RATE = 0.05
MLP_RATE = 0.04 * HID
F32 = jnp.float32
BF16 = jnp.bfloat16
MESH = pl.DeviceIdType.MESH


def kernel(
    table_hbm, state_hbm, grads_hbm, slots_hbm, rows_hbm, ids_hbm, count_hbm,
    inputs_hbm, cot_hbm, w1_hbm, w2_hbm,
    new_table, new_state, new_first, new_second,
    table, state_ref, lgrads, slots_ref, rows_ref, ids_ref, count_ref, w1, w2, left, right,
    dense, emb_recv, merged,
    g_sib, g_own, g_recv,
    r1x, r1y, r1z, t2x, t2y, t2z, r2x, r2y, r2z, r3y, r3z, w4x, w4y, w4z, f5x, f5y, f5z,
    in_sem, send_sem, recv_sem,
):
    rep = lax.axis_index("replica")
    tab = lax.axis_index("table")
    z, c = rep // C, lax.rem(rep, C)
    x, y = tab // Y, lax.rem(tab, Y)
    sib = 1 - c

    def at_x(d):
        return (rep, lax.rem(x + d, X) * Y + y)

    def at_y(d):
        return (rep, x * Y + lax.rem(y + d, Y))

    def at_z(d, core=c):
        return (lax.rem(z + d, Z) * C + core, tab)

    sibling = (z * C + sib, tab)

    opened, taken = {}, set()

    def send(src, dst, k, dev, whole):
        opened[k] = whole
        pltpu.make_async_remote_copy(
            src_ref=src, dst_ref=dst, send_sem=send_sem.at[k], recv_sem=recv_sem.at[k],
            device_id=dev, device_id_type=MESH,
        ).start()

    def take(k):
        taken.add(k)
        pltpu.make_async_copy(opened[k], opened[k], recv_sem.at[k]).wait()

    def finish():
        for k, whole in opened.items():
            if k not in taken:
                take(k)
            pltpu.make_async_copy(whole, whole, send_sem.at[k]).wait()

    barrier = pltpu.get_barrier_semaphore()
    peers = [at_x(d) for d in range(1, X)] + [at_y(d) for d in range(1, Y)]
    peers += [at_z(d) for d in range(1, Z)] + [at_z(d, sib) for d in range(Z)]
    for dev in peers:
        pl.semaphore_signal(barrier, inc=1, device_id=dev, device_id_type=MESH)

    parts = [pl.ds(k * CHUNK, CHUNK) for k in range(SAMPLES // CHUNK)]
    pairs = [
        (count_hbm, count_ref), (ids_hbm, ids_ref), (slots_hbm, slots_ref), (rows_hbm, rows_ref),
        (grads_hbm.at[0], lgrads), (w1_hbm, w1), (w2_hbm, w2),
    ]
    for rows in parts:
        pairs += [(inputs_hbm.at[rows], left.at[0, rows]), (cot_hbm.at[rows], right.at[1, rows])]
    pairs += [(state_hbm, state_ref), (table_hbm, table)]
    loads = [pltpu.make_async_copy(*pair, in_sem.at[k]) for k, pair in enumerate(pairs)]
    for load in loads:
        load.start()

    for load in loads[:5]:
        load.wait()
    count = count_ref[0, 0]
    slot_ids = slots_ref[...]
    position = jnp.where(slot_ids < count, slot_ids * BLOCK_ROWS + rows_ref[...], -1)
    lookup_grads = lgrads[...]
    slot_sums = []
    for k in range(SLOTS):
        target = lax.broadcasted_iota(jnp.int32, (BLOCK_ROWS, LOOKUPS), 0) + k * BLOCK_ROWS
        onehot = jnp.where(target == position, 1.0, 0.0).astype(BF16)
        found = jnp.dot(onehot, lookup_grads, preferred_element_type=F32)
        slot_sums.append(found.astype(BF16).astype(F32))
    for b in range(BLOCKS):
        block = jnp.zeros((BLOCK_ROWS, EMB), F32)
        for k in range(SLOTS):
            block += jnp.where((ids_ref[0, k] == b) & (k < count), 1.0, 0.0) * slot_sums[k]
        dense[pl.ds(b * BLOCK_ROWS, BLOCK_ROWS)] = block.astype(BF16)

    def share(zz, cc):
        return pl.ds(pl.multiple_of((cc * Z + zz) * SHARE, SHARE), SHARE)

    loads[5].wait()
    loads[6].wait()
    for k, rows in enumerate(parts):
        loads[7 + 2 * k].wait()
        loads[8 + 2 * k].wait()
        pre = jnp.dot(left[0, rows], w1[...], preferred_element_type=F32)
        back = lax.dot_general(
            right[1, rows], w2[...], (((1,), (1,)), ((), ())), preferred_element_type=F32
        )
        sig = jax.nn.sigmoid(pre)
        left[1, rows] = (pre * sig).astype(BF16)
        right[0, rows] = (back * sig * (1.0 + pre * (1.0 - sig))).astype(BF16)

    def grad(which, half):
        cols = pl.ds(half * 256, 256)
        return lax.dot_general(
            left[which], right[which, :, cols], (((0,), (0,)), ((), ())),
            preferred_element_type=F32,
        )

    for half in (1, 0):
        g = grad(sib, half)
        for k in range(2):
            g_sib[pl.ds(HID * (2 * half + k), HID)] = g[:, 128 * k:128 * k + 128]
    pl.semaphore_wait(barrier, len(peers))
    for k in (2, 3, 0, 1):
        rows = pl.ds(HID * k, HID)
        send(g_sib.at[rows], g_recv.at[rows], PAIR + k, sibling, g_recv.at[rows])

    for d in FAR[Z] + (0,):
        for core in (c, sib):
            if d == 0 and core is c:
                continue
            send(
                dense.at[share(lax.rem(z + d, Z), core)], emb_recv.at[rep], 0, at_z(d, core),
                emb_recv.at[pl.ds(0, Z * C - 1)],
            )
    emb_recv[rep] = dense[share(z, c)]

    for half in (1, 0):
        g = grad(c, half)
        for k in range(2):
            g_own[pl.ds(HID * (2 * half + k), HID)] = g[:, 128 * k:128 * k + 128]

    def piece(k, rows, start=0):
        return pl.ds(pl.multiple_of(start + k * rows, 8), rows)

    take(PAIR + 2)
    take(PAIR + 3)
    g_own[2 * HID:] = g_own[2 * HID:] + g_recv[2 * HID:]
    for d in FAR[Y]:
        rows = piece(lax.rem(y + d, Y), PB, AT_B)
        send(g_own.at[rows], r1y.at[d - 1], 5, at_y(d), r1y)
        rows = piece(lax.rem(z + d, Z), PZ, AT_Z)
        send(g_own.at[rows], r1z.at[d - 1], 6, at_z(d), r1z)
    take(PAIR)
    take(PAIR + 1)
    g_own[:2 * HID] = g_own[:2 * HID] + g_recv[:2 * HID]
    for d in FAR[X]:
        rows = piece(lax.rem(x + d, X), PA)
        send(g_own.at[rows], r1x.at[d - 1, pl.ds(0, PA)], 4, at_x(d), r1x)
        rows = piece(lax.rem(x + d, X), PD, AT_D)
        send(g_own.at[rows], r1x.at[d - 1, pl.ds(PA, PD)], 4, at_x(d), r1x)

    def summed(ref, n, first):
        for k in range(n):
            first = first + ref[k]
        return first

    take(0)
    total = emb_recv[0].astype(F32)
    for k in range(1, Z * C):
        total += emb_recv[k].astype(F32)
    merged[share(z, c)] = total
    r3z[z, QA + QB:QA + QB + 8] = jnp.sum((total * total).reshape(SHARE // 8, 8, EMB), axis=0)

    take(4)
    s = g_own[piece(x, PA)]
    for k in range(X - 1):
        s = s + r1x[k, 0:PA]
    t2y[...] = s.reshape(Y, QA, 128)
    s = g_own[piece(x, PD, AT_D)]
    for k in range(X - 1):
        s = s + r1x[k, PA:PX]
    t2z[...] = s.reshape(Z, QD, 128)
    for d in FAR[Y]:
        send(t2y.at[lax.rem(y + d, Y)], r2y.at[d - 1], 9, at_y(d), r2y)
        send(t2z.at[lax.rem(z + d, Z)], r2z.at[d - 1], 8, at_z(d), r2z)
    for d in (2, 6, 1, 7):
        send(
            merged.at[share(z, c)], merged.at[share(z, c)], 3, at_z(d), merged.at[pl.ds(0, 4 * SHARE)]
        )

    take(5)
    t2x[:, 0:QB] = summed(r1y, Y - 1, g_own[piece(y, PB, AT_B)]).reshape(X, QB, 128)
    take(6)
    t2x[:, QB:QB + QZ] = summed(r1z, Z - 1, g_own[piece(z, PZ, AT_Z)]).reshape(X, QZ, 128)
    for d in FAR[X]:
        send(t2x.at[lax.rem(x + d, X)], r2x.at[d - 1], 7, at_x(d), r2x)

    take(9)
    r3z[z, 0:QA] = summed(r2y, Y - 1, t2y[y])
    take(8)
    r3y[y, 0:QD] = summed(r2z, Z - 1, t2z[z])
    take(7)
    s = summed(r2x, X - 1, t2x[x])
    r3z[z, QA:QA + QB] = s[0:QB]
    r3y[y, QD:QD + QZ] = s[QB:QB + QZ]
    for d in FAR[Y]:
        send(r3z.at[z], r3z.at[z], 11, at_z(d), r3z.at[pl.ds(0, Z - 1)])
        send(r3y.at[y], r3y.at[y], 10, at_y(d), r3y.at[pl.ds(0, Y - 1)])

    take(11)
    s = summed(r3z, Z, 0.0)
    w4y[y, 0:QA] = s[0:QA]
    w4y[y, QA:QA + 8] = s[QA + QB:QA + QB + 8]
    w4x[x, 0:QB] = s[QA:QA + QB]
    for d in FAR[Y]:
        send(w4y.at[y], w4y.at[y], 14, at_y(d), w4y.at[pl.ds(0, Y - 1)])
    take(10)
    s = summed(r3y, Y, 0.0)
    w4z[z] = s[0:QD]
    w4x[x, QB:QB + QZ] = s[QD:QD + QZ]
    for d in FAR[X]:
        send(w4x.at[x], w4x.at[x], 12, at_x(d), w4x.at[pl.ds(0, X - 1)])
    for d in FAR[Z]:
        send(w4z.at[z], w4z.at[z], 13, at_z(d), w4z.at[pl.ds(0, Z - 1)])

    take(3)
    up, down = share(lax.rem(z + 2, Z), c), share(lax.rem(z + 6, Z), c)
    start = (c * Z) * SHARE
    up_half = pl.ds(pl.multiple_of(start + lax.rem(z + 2, Z) * SHARE, 32), SHARE // 2)
    down_half = pl.ds(
        pl.multiple_of(start + lax.rem(z + 6, Z) * SHARE + SHARE // 2, 32), SHARE // 2
    )
    for rows, d in ((up_half, 6), (down_half, 2), (up, 7), (down, 1)):
        send(merged.at[rows], merged.at[rows], 22, at_z(d), merged.at[pl.ds(0, 3 * SHARE)])

    take(12)
    f5y[c, y] = w4x[:, 0:QB].reshape(PB, 128)
    f5z[c, z] = w4x[:, QB:QB + QZ].reshape(PZ, 128)
    for d in FAR[Y]:
        send(f5y.at[c, y], f5y.at[c, y], 15, at_y(d), f5y.at[0, pl.ds(0, Y - 1)])
        send(f5z.at[c, z], f5z.at[c, z], 17, at_z(d), f5z.at[0, pl.ds(0, Z - 1)])

    half_rows = piece(c, ROWS // 2)
    take(22)
    send(merged.at[half_rows], merged.at[half_rows], 18, sibling, merged.at[half_rows])
    lane = lax.broadcasted_iota(jnp.int32, (BLOCK_ROWS, 128), 1)

    def squares_of(core):
        found = jnp.zeros((BLOCK_ROWS, 128), F32)
        for k in range(BLOCKS // C):
            b = core * (BLOCKS // C) + k
            m = merged[piece(b, BLOCK_ROWS)]
            found = jnp.where(lane == b, jnp.sum(m * m, axis=1, keepdims=True), found)
        return found

    take(14)
    f5x[c, x, 0:PA] = w4y[:, 0:QA].reshape(PA, 128)
    f5x[c, x, PX:PX + 8] = jnp.sum(w4y[:, QA:QA + 8], axis=0)
    take(13)
    f5x[c, x, PA:PX] = w4z[...].reshape(PD, 128)
    for d in FAR[X]:
        send(f5x.at[c, x], f5x.at[c, x], 16, at_x(d), f5x.at[0, pl.ds(0, X - 1)])

    squares = squares_of(c)
    take(18)
    squares = (squares + squares_of(sib)) * (1.0 / EMB)
    squares_row = jnp.transpose(squares)[0:BLOCKS]
    loads[-2].wait()
    state_row = state_ref[...]
    state_col = jnp.transpose(
        jnp.concatenate([state_row, jnp.zeros((BLOCK_ROWS - BLOCKS, 128), F32)], axis=0)
    )

    def squared(core):
        found = jnp.zeros((32, 128), F32)
        for ref, n, rows in ((f5x, X, PX), (f5y, Y, PB), (f5z, Z, PZ)):
            for k in range(n):
                for q in range(rows // 32):
                    v = ref[core, k, 32 * q:32 * q + 32]
                    found += v * v
        return found

    take(16)
    send(f5x.at[c], f5x.at[c], 19, sibling, f5x.at[0])
    take(15)
    send(f5y.at[c], f5y.at[c], 20, sibling, f5y.at[0])
    take(17)
    send(f5z.at[c], f5z.at[c], 21, sibling, f5z.at[0])
    mine = squared(c)
    loads[-1].wait()
    take(19)
    take(20)
    take(21)
    other = squared(sib)

    emb = f5x[:, :, PX:PX + 8]
    total = jnp.sum(mine + other, keepdims=True)
    total = total + jnp.sum(jnp.sum(emb, axis=(0, 1)), keepdims=True)
    clip = jnp.minimum(1.0, 1.0 / (jnp.sqrt(total) + 1e-06))

    clip_sq = clip * clip
    scale = (EMB_RATE * clip) / jnp.sqrt(state_col + clip_sq * squares)
    for b in range(BLOCKS):
        rows = pl.ds(b * BLOCK_ROWS, BLOCK_ROWS)
        new_table[rows] = table[rows] - merged[rows] * scale[:, b:b + 1]
    new_state[...] = state_row + clip_sq * squares_row
    rate = MLP_RATE * clip
    spans = [(f5x, k, 0, PA * k, PA) for k in range(X)]
    spans += [(f5x, k, PA, AT_D + PD * k, PD) for k in range(X)]
    spans += [(f5y, k, 0, AT_B + PB * k, PB) for k in range(Y)]
    spans += [(f5z, k, 0, AT_Z + PZ * k, PZ) for k in range(Z)]
    for core, (w, out) in enumerate(((w1, new_first), (w2, new_second))):
        for ref, k, start, row, count in spans:
            for q in range(0, count, 32):
                rows = pl.ds((row + q) % HID, 32)
                cols = pl.ds((row + q) // HID * 128, 128)
                g = ref[core, k, start + q:start + q + 32]
                out[rows, cols] = (w[rows, cols].astype(F32) - rate * g).astype(BF16)
    finish()


def hand_over(*refs):
    *arrays, sem = refs
    n = len(arrays) // 2
    copies = [pltpu.make_async_copy(arrays[k], arrays[n + k], sem.at[k]) for k in range(n)]
    for copy in copies:
        copy.start()
    for copy in copies:
        copy.wait()


def on_device(
    table, row_state, lookup_grads, lookup_slots, lookup_rows, block_ids, block_counts,
    inputs, cotangent, w_first, w_second,
):
    hbm = pl.BlockSpec(memory_space=pl.ANY)
    vmem = pl.BlockSpec(memory_space=pltpu.VMEM)
    shapes = (
        jax.ShapeDtypeStruct((ROWS, EMB), F32),
        jax.ShapeDtypeStruct((BLOCKS, BLOCK_ROWS), F32),
        jax.ShapeDtypeStruct((HID, HID), BF16),
        jax.ShapeDtypeStruct((HID, HID), BF16),
    )
    results = pl.pallas_call(
        kernel,
        out_shape=tuple(pltpu.VMEM(a.shape, a.dtype) for a in shapes),
        in_specs=[hbm] * 11,
        out_specs=(vmem,) * 4,
        scratch_shapes=[
            pltpu.VMEM((ROWS, EMB), F32),
            pltpu.VMEM((BLOCKS, BLOCK_ROWS), F32),
            pltpu.VMEM((LOOKUPS, EMB), BF16),
            pltpu.VMEM((1, LOOKUPS), jnp.int32),
            pltpu.VMEM((1, LOOKUPS), jnp.int32),
            pltpu.SMEM((1, SLOTS), jnp.int32),
            pltpu.SMEM((1, 1), jnp.int32),
            pltpu.VMEM((HID, HID), BF16),
            pltpu.VMEM((HID, HID), BF16),
            pltpu.VMEM((2, SAMPLES, HID), BF16),
            pltpu.VMEM((2, SAMPLES, HID), BF16),
            pltpu.VMEM((ROWS, EMB), BF16),
            pltpu.VMEM((Z * C, SHARE, EMB), BF16),
            pltpu.VMEM((ROWS, EMB), F32),
            pltpu.VMEM((4 * HID, 128), F32),
            pltpu.VMEM((4 * HID, 128), F32),
            pltpu.VMEM((4 * HID, 128), F32),
            pltpu.VMEM((X - 1, PX, 128), F32),
            pltpu.VMEM((Y - 1, PB, 128), F32),
            pltpu.VMEM((Z - 1, PZ, 128), F32),
            pltpu.VMEM((X, QB + QZ, 128), F32),
            pltpu.VMEM((Y, QA, 128), F32),
            pltpu.VMEM((Z, QD, 128), F32),
            pltpu.VMEM((X - 1, QB + QZ, 128), F32),
            pltpu.VMEM((Y - 1, QA, 128), F32),
            pltpu.VMEM((Z - 1, QD, 128), F32),
            pltpu.VMEM((Y, QD + QZ, 128), F32),
            pltpu.VMEM((Z, QA + QB + 8, 128), F32),
            pltpu.VMEM((X, QB + QZ, 128), F32),
            pltpu.VMEM((Y, QA + 8, 128), F32),
            pltpu.VMEM((Z, QD, 128), F32),
            pltpu.VMEM((C, X, PX + 8, 128), F32),
            pltpu.VMEM((C, Y, PB, 128), F32),
            pltpu.VMEM((C, Z, PZ, 128), F32),
            pltpu.SemaphoreType.DMA((9 + 2 * SAMPLES // CHUNK,)),
            pltpu.SemaphoreType.DMA((27,)),
            pltpu.SemaphoreType.DMA((27,)),
        ],
        compiler_params=pltpu.CompilerParams(
            collective_id=0, has_side_effects=True, vmem_limit_bytes=60 * 2**20
        ),
        cost_estimate=pl.CostEstimate(
            flops=2_400_000_000, bytes_accessed=6 * 2**20, transcendentals=2**20
        ),
        name="step",
    )(
        table, row_state.reshape(BLOCKS, BLOCK_ROWS), lookup_grads, lookup_slots, lookup_rows,
        block_ids, block_counts, inputs, cotangent, w_first, w_second,
    )
    new_table, new_state, new_first, new_second = pl.pallas_call(
        hand_over,
        out_shape=shapes,
        in_specs=[vmem] * 4,
        out_specs=(hbm,) * 4,
        scratch_shapes=[pltpu.SemaphoreType.DMA((4,))],
        compiler_params=pltpu.CompilerParams(vmem_limit_bytes=16 * 2**20),
        name="hand_over",
    )(*results)
    return (new_table, new_state.reshape(ROWS), new_first, new_second)


def solution(mesh):
    placed = (
        P("table", None),
        P("table"),
        P("replica", "table", None),
        P("replica", "table"),
        P("replica", "table"),
        P("replica", "table"),
        P("replica", "table"),
        P(("replica", "table"), None),
        P(("replica", "table"), None),
        P(),
        P(),
    )
    return jax.shard_map(
        on_device,
        mesh=mesh,
        in_specs=placed,
        out_specs=(P("table", None), P("table"), P(), P()),
        check_vma=False,
    )
```
